32 devices in a mesh: seq: 8 (over z, y), head: 4 (over x, core).
Axes of the slice: x: 2, y: 2, z: 4, core: 2. Of those that a mesh axis runs over, the one named last changes fastest.
Arguments:
- query_rows: bfloat16 [1024, 2048], P('seq', 'head'), may hold values from -6 to 6
- key_rows: bfloat16 [1024, 2048], P('seq', 'head'), may hold values from -0.52734375 to 0.52734375
- value_rows: bfloat16 [1024, 2048], P('seq', 'head'), may hold values from -6 to 6
- ridge_reg: float32 [16], P('head'), may hold values from 0.5 to 4
- out_weight: bfloat16 [2048, 2048], P('head'), may hold values from -0.125 to 0.125
- out_grad: bfloat16 [1024, 2048], P('seq', 'head'), may hold values from -8 to 8
- doc_ids: int32 [1024], P('seq'), may hold values from 0 to 3, never falling along the last dimension, each value on 1 to 512 neighbouring positions
Outputs:
- layer_out: bfloat16 [1024, 2048], P('seq', 'head')
- grad_queries: bfloat16 [1024, 2048], P('seq', 'head')
- grad_keys: bfloat16 [1024, 2048], P('seq', 'head')
- grad_values: bfloat16 [1024, 2048], P('seq', 'head')
- grad_weight: float32 [2048, 2048], P('seq', 'head')
The draws below stay inside these ranges and needn't reach their ends.
Inputs may be any that keep to these rules, and one draw needn't show every extreme that they name: `doc_ids`: document numbers never fall along the tokens; every number occurs, each document has 1 to 512 tokens and one has exactly 512.
All inputs are finite; a program needn't handle non-finite values.
Results may differ from the reference program's by a relative error of at most 0.018.
Values may be sent and summed in bfloat16 or wider, within the bound.
No kernel may reach another device: no remote copies, remote signals or barrier semaphores. Data moves between devices by JAX's collectives and lax.ppermute only.
A program may use at most 128 MiB of HBM per device.

```python
import math
import jax
import jax.numpy as jnp
import numpy as np
from jax import lax

D = 2048
HEADS = 16
DH = 128
PIECE = 128
CG_STEPS = 4
TOKENS = 1024
DOCS = 4
DOC_MOST = 512


def strengthened(values, own_key, source, target, shards_of, factor):
    owner, partner = [(jnp.arange(values.shape[position]) // (values.shape[position] // shards_of)).reshape([-1 if axis == position else 1 for axis in range(values.ndim)]) for position in (source, target)]
    chosen = jax.random.permutation(own_key, shards_of)[partner]
    strong = (owner == chosen) | (owner == (partner + shards_of // 2) % shards_of)
    return jnp.where(strong, factor * values, values)


def block_levels(rng, dims, cuts, least, top_value):
    level, own = 1.0, jax.random.fold_in(rng, 6)
    for dim, parts in cuts:
        draws = jnp.exp(jax.random.uniform(jax.random.fold_in(own, dim), (parts,), jnp.float32, least / len(cuts), top_value / len(cuts)))
        level = level * jnp.repeat(draws, dims[dim] // parts).reshape([-1 if axis == dim else 1 for axis in range(len(dims))])
    return level


def profile(count, total, bound, skew):
    loads = [(1 << 20) // math.isqrt(standing ** skew) + 1 for standing in range(2, count + 1)]
    rest, holding = total - bound - (count - 1), [1] * (count - 1)
    while rest > 0:
        candidates = [i for i in range(count - 1) if holding[i] < bound]
        pool, remaining = sum([loads[i] for i in candidates]), rest
        for i in candidates:
            addition = min(bound - holding[i], max(1, remaining * loads[i] // pool), rest)
            holding[i] = holding[i] + addition
            rest = rest - addition
    return np.array([bound] + holding)


def uneven_parts(key, number_of, total, limit, slope):
    if number_of == 2:
        one = jax.random.randint(key, (), max(1, total - limit), min(limit, total - 1) + 1)
        return jnp.stack([one, total - one])
    lengths = jnp.asarray(profile(number_of, total, limit, slope), jnp.int32)
    couples = (number_of - 1) // 2
    giver, receiver = lengths[1:1 + 2 * couples:2], lengths[2:2 + 2 * couples:2]
    slack = jnp.minimum(giver - 1, limit - receiver)
    moved = jax.random.randint(jax.random.fold_in(key, 1), (couples,), 0, 1 << 20) % (slack + 1)
    lengths = lengths.at[1:1 + 2 * couples:2].set(giver - moved).at[2:2 + 2 * couples:2].set(receiver + moved)
    return lengths[jax.random.permutation(jax.random.fold_in(key, 2), number_of)]


def normal_values(own_key, dims, scale, bound, cuts=(), dtype=jnp.bfloat16):
    values = scale * jax.random.normal(own_key, dims, jnp.float32)
    if cuts:
        values = values * block_levels(own_key, dims, cuts, -0.22, 0.18)
    return jnp.clip(values, -bound, bound).astype(dtype)


def bell_draw_with(key, dims, deviation, reach, split, heavy, held_as=jnp.bfloat16):
    values = deviation * jax.random.normal(key, dims, jnp.float32)
    if split:
        values = values * block_levels(key, dims, split, -0.22, 0.18)
    return jnp.clip(strengthened(values, jax.random.fold_in(key, 3), *heavy), -reach, reach).astype(held_as)


def setup_inputs(seed: int = 0) -> dict:
    splits = jax.random.split(jax.random.key(seed), 8)
    query_rows = normal_values(splits[0], (TOKENS, HEADS * DH), 1.0, 6.0, ((0, 8), (1, 4)))
    key_rows = normal_values(splits[1], (TOKENS, HEADS * DH), (DH ** -0.5), 0.52734375, ((0, 8), (1, 4)))
    value_rows = normal_values(splits[2], (TOKENS, HEADS * DH), 1.0, 6.0, ((0, 8), (1, 4)))
    ridge_reg = jnp.clip(jnp.exp(math.log(4.0) - 2.0794415 * jax.random.uniform(splits[3], (HEADS,), jnp.float32) ** block_levels(splits[3], (HEADS,), ((0, 4),), -0.2, 0.2)), 0.5, 4.0)
    out_weight = normal_values(splits[4], (HEADS * DH, D), (HEADS * DH) ** -0.5, 0.125, ((0, 4),))
    out_grad = bell_draw_with(splits[5], (TOKENS, D), 1.0, 8.0, ((0, 8), (1, 4)), (0, 1, 8, 2.0))
    doc_ids = jnp.searchsorted(jnp.cumsum(uneven_parts(splits[6], DOCS, TOKENS, DOC_MOST, 2)), jnp.arange(TOKENS), side="right").astype(jnp.int32)
    return dict(query_rows=query_rows, key_rows=key_rows, value_rows=value_rows, ridge_reg=ridge_reg, out_weight=out_weight, out_grad=out_grad, doc_ids=doc_ids)


epsilon = 1e-6


def matmul_high(left_side, right_side):
    return jnp.dot(left_side, right_side, precision=lax.Precision.HIGHEST, preferred_element_type=jnp.float32)


def causal_mask(labels):
    length = labels.shape[0]
    row_idx = lax.broadcasted_iota(jnp.int32, (length, length), 0)
    col_idx = lax.broadcasted_iota(jnp.int32, (length, length), 1)
    return ((labels[:, None] == labels[None, :]) & (col_idx <= row_idx)).astype(jnp.float32)


def conj_solve(target, key_rows, same_doc, carried, gram_in, ridge_reg):
    def apply_matrix(direction):
        scores = matmul_high(direction, key_rows.T) * same_doc
        return carried[:, None] * matmul_high(direction, gram_in) + matmul_high(scores, key_rows) + ridge_reg * direction

    solution = jnp.zeros_like(target)
    residual = target
    direction = target
    res_sq = jnp.sum(residual * residual, axis=1, keepdims=True)
    for number in range(CG_STEPS):
        applied = apply_matrix(direction)
        step_size = res_sq / (jnp.sum(direction * applied, axis=1, keepdims=True) + epsilon)
        solution = solution + step_size * direction
        residual = residual - step_size * applied
        new_sq = jnp.sum(residual * residual, axis=1, keepdims=True)
        direction = residual + (new_sq / (res_sq + epsilon)) * direction
        res_sq = new_sq
    return solution


def head_forward(query_rows, key_rows, value_rows, same_doc, carried, gram_in, value_in, ridge_reg):
    solution = conj_solve(query_rows, key_rows, same_doc, carried, gram_in, ridge_reg)
    score_one = matmul_high(solution, key_rows.T) * same_doc
    output = carried[:, None] * matmul_high(solution, value_in.T) + matmul_high(score_one, value_rows)
    return solution, output


def head_dual(key_rows, value_rows, same_doc, carried, head_rows, gram_in, value_in, ridge_reg, solution, out_cot):
    score_two = matmul_high(out_cot, value_rows.T) * same_doc
    target = carried[:, None] * matmul_high(out_cot, value_in) + matmul_high(score_two, key_rows)
    dual_sol = conj_solve(target, key_rows, same_doc, carried, gram_in, ridge_reg)
    state_part = matmul_high(out_cot.T, head_rows[:, None] * solution)
    cross_sum = matmul_high(dual_sol.T, head_rows[:, None] * solution)
    return dual_sol, state_part, cross_sum + cross_sum.T, score_two


def head_grads(key_rows, value_rows, same_doc, later_rows, solution, out_cot, dual_sol, score_two, grad_state, gram_grad):
    score_one = matmul_high(solution, key_rows.T) * same_doc
    score_three = matmul_high(dual_sol, key_rows.T) * same_doc
    grad_v = later_rows[:, None] * matmul_high(key_rows, grad_state.T) + matmul_high(score_one.T, out_cot)
    grad_k = later_rows[:, None] * (matmul_high(value_rows, grad_state) - matmul_high(key_rows, gram_grad))
    grad_k = grad_k + matmul_high(score_two.T, solution) - matmul_high(score_one.T, dual_sol) - matmul_high(score_three.T, solution)
    return grad_k, grad_v


def split_heads(array):
    return array.astype(jnp.float32).reshape(-1, PIECE, HEADS, DH).transpose(0, 2, 1, 3)


def join_heads(array):
    return array.transpose(0, 2, 1, 3).reshape(-1, HEADS * DH)


def reference(query_rows, key_rows, value_rows, ridge_reg, out_weight, out_grad, doc_ids):
    query_h = split_heads(query_rows)
    key_h = split_heads(key_rows)
    value_h = split_heads(value_rows)
    label_rows = doc_ids.reshape(-1, PIECE)
    zero_state = jnp.zeros((HEADS, DH, DH), jnp.float32)
    start_state = (jnp.array(-1, jnp.int32), zero_state, zero_state)

    def forward_piece(carry, inputs):
        label_in, gram_in, value_in = carry
        query_p, key_p, value_p, labels = inputs
        same_doc = causal_mask(labels)
        carried = (labels == label_in).astype(jnp.float32)
        solution, output = jax.vmap(head_forward, in_axes=(0, 0, 0, None, None, 0, 0, 0))(
            query_p, key_p, value_p, same_doc, carried, gram_in, value_in, ridge_reg)
        tail_rows = (labels == labels[-1]).astype(jnp.float32)[None, :, None]
        gram_tail = jnp.einsum("hpk,hpl->hkl", key_p * tail_rows, key_p, precision=lax.Precision.HIGHEST, preferred_element_type=jnp.float32)
        value_tail = jnp.einsum("hpv,hpk->hvk", value_p * tail_rows, key_p, precision=lax.Precision.HIGHEST, preferred_element_type=jnp.float32)
        joined = ((labels[0] == labels[-1]) & (labels[-1] == label_in)).astype(jnp.float32)
        new_carry = (labels[-1], gram_tail + joined * gram_in, value_tail + joined * value_in)
        return new_carry, (solution, output, gram_in, value_in, label_in)

    final_state, saved = lax.scan(forward_piece, start_state, (query_h, key_h, value_h, label_rows))
    solution_all, output_all, gram_all, value_all, label_all = saved
    mixed = join_heads(output_all).astype(jnp.bfloat16)
    layer_out = jnp.dot(mixed, out_weight, preferred_element_type=jnp.float32).astype(jnp.bfloat16)
    grad_weight = jnp.dot(out_grad.T, mixed, preferred_element_type=jnp.float32)
    out_cot_all = split_heads(jnp.dot(out_grad, out_weight.T, preferred_element_type=jnp.float32))

    def backward_piece(carry, inputs):
        label_after, grad_state, gram_grad = carry
        key_p, value_p, labels, solution, out_cot, gram_in, value_in, label_in = inputs
        same_doc = causal_mask(labels)
        carried = (labels == label_in).astype(jnp.float32)
        head_rows = (labels == labels[0]).astype(jnp.float32)
        later_rows = (labels == label_after).astype(jnp.float32)
        dual_sol, state_part, gram_part, score_two = jax.vmap(head_dual, in_axes=(0, 0, None, None, None, 0, 0, 0, 0, 0))(
            key_p, value_p, same_doc, carried, head_rows, gram_in, value_in, ridge_reg, solution, out_cot)
        grad_k, grad_v = jax.vmap(head_grads, in_axes=(0, 0, None, None, 0, 0, 0, 0, 0, 0))(
            key_p, value_p, same_doc, later_rows, solution, out_cot, dual_sol, score_two, grad_state, gram_grad)
        joined = ((labels[0] == labels[-1]) & (labels[0] == label_after)).astype(jnp.float32)
        new_carry = (labels[0], state_part + joined * grad_state, gram_part + joined * gram_grad)
        return new_carry, (dual_sol, grad_k, grad_v)

    end_state, grads = lax.scan(backward_piece, start_state,
                                (key_h, value_h, label_rows, solution_all, out_cot_all, gram_all, value_all, label_all),
                                reverse=True)
    dual_all, grad_k_all, grad_v_all = grads
    grad_queries = join_heads(dual_all).astype(jnp.bfloat16)
    grad_keys = join_heads(grad_k_all).astype(jnp.bfloat16)
    grad_values = join_heads(grad_v_all).astype(jnp.bfloat16)
    return (layer_out, grad_queries, grad_keys, grad_values, grad_weight)
```

```python
import functools

import jax
import jax.numpy as jnp
from jax import lax
from jax.experimental import pallas as pl
from jax.experimental.pallas import tpu as pltpu
from jax.sharding import PartitionSpec as P

CG_STEPS = 4
EPSILON = 1e-06
LABEL_ROWS = 16
F32 = jnp.float32
BF16 = jnp.bfloat16
VMEM_LIMIT = 48 * 1024 * 1024


def mm(a, b):
    return lax.dot_general(a, b, (((1,), (0,)), ((), ())), preferred_element_type=F32)


def mm_nt(a, b):
    return lax.dot_general(a, b, (((1,), (1,)), ((), ())), preferred_element_type=F32)


def mm_tn(a, b):
    return lax.dot_general(a, b, (((0,), (0,)), ((), ())), preferred_element_type=F32)


def kernel_call(body, out_shape, operands, flops, name, smem=()):
    in_specs = [
        pl.BlockSpec(memory_space=pltpu.SMEM if i in smem else pltpu.VMEM)
        for i in range(len(operands))
    ]
    nbytes = sum(o.size * o.dtype.itemsize for o in operands)
    nbytes += sum(o.size * o.dtype.itemsize for o in out_shape)
    return pl.pallas_call(
        body,
        out_shape=out_shape,
        in_specs=in_specs,
        out_specs=[pl.BlockSpec(memory_space=pltpu.VMEM)] * len(out_shape),
        compiler_params=pltpu.CompilerParams(vmem_limit_bytes=VMEM_LIMIT),
        cost_estimate=pl.CostEstimate(flops=flops, bytes_accessed=nbytes, transcendentals=0),
        name=name,
    )(*operands)


def label_grids(doc_ref, piece):
    across = jnp.broadcast_to(doc_ref[...], (piece, piece))
    return across, across.T


def document_mask(across, down):
    row = lax.broadcasted_iota(jnp.int32, across.shape, 0)
    col = lax.broadcasted_iota(jnp.int32, across.shape, 1)
    return (across == down) & (col <= row)


def tail_body(heads, width, doc_ref, key_ref, value_ref, out_ref):
    piece = key_ref.shape[0]
    across, down = label_grids(doc_ref, piece)
    last = jnp.max(across, axis=1, keepdims=True)
    tail = (down == last).astype(F32).astype(BF16)
    states = heads * width
    for h in range(heads):
        cols = slice(h * width, (h + 1) * width)
        key_h = key_ref[:, cols]
        masked = key_h * tail[:, :width]
        out_ref[h * width : (h + 1) * width, :] = mm_tn(key_h, masked).astype(BF16)
        out_ref[states + h * width : states + (h + 1) * width, :] = mm_tn(
            value_ref[:, cols], masked
        ).astype(BF16)
    label = (last[:LABEL_ROWS] + 1).astype(F32)
    out_ref[2 * states :, :] = jnp.broadcast_to(label, (LABEL_ROWS, width)).astype(BF16)


def cot_body(count, shard, place_ref, *refs):
    cots, weight_ref, cot_ref, full_ref = refs[:count], refs[count], refs[count + 1], refs[count + 2]
    me = place_ref[1]
    total = None
    for b in range(count):
        owner = jnp.bitwise_xor(me, b)
        cols = pl.ds(pl.multiple_of(owner * shard, shard), shard)
        block = cots[b][...]
        full_ref[:, cols] = block
        part = mm_nt(block, weight_ref[:, cols])
        total = part if total is None else total + part
    cot_ref[...] = total.astype(BF16)


def project_body(count, shard, place_ref, mixed_ref, weight_ref, own_ref, *send_refs):
    me = place_ref[1]
    mixed = mixed_ref[...]
    for b in range(count):
        owner = jnp.bitwise_xor(me, b)
        cols = pl.ds(pl.multiple_of(owner * shard, shard), shard)
        part = mm(mixed, weight_ref[:, cols])
        if b == 0:
            own_ref[...] = part
        else:
            send_refs[b - 1][...] = part.astype(BF16)


def solve_body(
    heads,
    width,
    ridge_ref,
    doc_ref,
    query_ref,
    key_ref,
    value_ref,
    cot_ref,
    near_ref,
    far_ref,
    sol_ref,
    dual_ref,
    mixed_ref,
    out_ref,
):
    piece = key_ref.shape[0]
    states = heads * width
    across, down = label_grids(doc_ref, piece)
    same = document_mask(across, down).astype(F32)
    same_two = jnp.concatenate([same, same], axis=0)
    first = jnp.min(across, axis=1, keepdims=True)
    head_rows = (down == first)[:, :width].astype(F32)
    near_label = near_ref[2 * states : 2 * states + LABEL_ROWS, :].astype(F32)[0:1, :]
    far_label = far_ref[2 * states : 2 * states + LABEL_ROWS, :].astype(F32)[0:1, :]
    joined = jnp.broadcast_to((near_label == far_label).astype(F32), (width, width))
    carried = ((down + 1).astype(F32)[:, :width] == near_label).astype(F32)
    carried_two = jnp.concatenate([carried, carried], axis=0)

    def state(index):
        rows = slice(index * width, (index + 1) * width)
        return (near_ref[rows, :].astype(F32) + joined * far_ref[rows, :].astype(F32)).astype(BF16)

    keys, rhs_keys, values, grams, solutions, residuals, directions, squares = ([] for _ in range(8))
    value_states = []
    for h in range(heads):
        cols = slice(h * width, (h + 1) * width)
        key_h = key_ref[:, cols]
        value_h = value_ref[:, cols]
        value_state = state(heads + h)
        cot_h = cot_ref[:, cols]
        both = mm(cot_h, jnp.concatenate([value_h.T, value_state], axis=1))
        scores = (both[:, :piece] * same).astype(BF16)
        target = carried * both[:, piece:] + mm(scores, key_h)
        start = jnp.concatenate([query_ref[:, cols].astype(F32), target], axis=0)
        keys.append(key_h)
        values.append(value_h)
        value_states.append(value_state)
        rhs_keys.append(jnp.concatenate([key_h.T, state(h)], axis=1))
        solutions.append(jnp.zeros_like(start))
        residuals.append(start)
        directions.append(start)
        squares.append(jnp.sum(start * start, axis=1, keepdims=True))
    for step in range(CG_STEPS):
        for h in range(heads):
            p = directions[h]
            both = mm(p.astype(BF16), rhs_keys[h])
            scores = (both[:, :piece] * same_two).astype(BF16)
            applied = carried_two * both[:, piece:] + mm(scores, keys[h]) + ridge_ref[h] * p
            size = squares[h] / (jnp.sum(p * applied, axis=1, keepdims=True) + EPSILON)
            solutions[h] = solutions[h] + size * p
            if step + 1 < CG_STEPS:
                residuals[h] = residuals[h] - size * applied
                new_sq = jnp.sum(residuals[h] * residuals[h], axis=1, keepdims=True)
                directions[h] = residuals[h] + new_sq / (squares[h] + EPSILON) * p
                squares[h] = new_sq
    for h in range(heads):
        cols = slice(h * width, (h + 1) * width)
        sol = solutions[h][:piece]
        sol_b = sol.astype(BF16)
        dual_b = solutions[h][piece:].astype(BF16)
        both = mm(sol_b, jnp.concatenate([rhs_keys[h][:, :piece], value_states[h].T], axis=1))
        scores = (both[:, :piece] * same).astype(BF16)
        output = carried * both[:, piece:] + mm(scores, values[h])
        mixed_ref[:, cols] = output.astype(BF16)
        sol_ref[:, cols] = sol_b
        dual_ref[:, cols] = dual_b
        masked = (head_rows * sol).astype(BF16)
        out_ref[h * width : (h + 1) * width, :] = mm_tn(cot_ref[:, cols], masked).astype(BF16)
        cross = mm_tn(dual_b, masked)
        out_ref[states + h * width : states + (h + 1) * width, :] = (cross + cross.T).astype(BF16)
    label = (first[:LABEL_ROWS] + 1).astype(F32)
    out_ref[2 * states :, :] = jnp.broadcast_to(label, (LABEL_ROWS, width)).astype(BF16)


def local_grads_body(
    heads, width, doc_ref, key_ref, value_ref, cot_ref, sol_ref, dual_ref, grad_k_ref, grad_v_ref
):
    piece = key_ref.shape[0]
    across, down = label_grids(doc_ref, piece)
    same = document_mask(across, down).astype(F32)
    same_two = jnp.concatenate([same, same], axis=0)
    for h in range(heads):
        cols = slice(h * width, (h + 1) * width)
        key_h, value_h, cot_h = key_ref[:, cols], value_ref[:, cols], cot_ref[:, cols]
        sol, dual = sol_ref[:, cols], dual_ref[:, cols]
        score_two = (mm_nt(cot_h, value_h) * same).astype(BF16)
        pair = (mm_nt(jnp.concatenate([sol, dual], axis=0), key_h) * same_two).astype(BF16)
        score_one, score_three = pair[:piece], pair[piece:]
        grad_v_ref[:, cols] = mm_tn(score_one, cot_h)
        grad_k_ref[:, cols] = mm_tn(
            jnp.concatenate([score_two, -score_three, -score_one], axis=0),
            jnp.concatenate([sol, sol, dual], axis=0),
        )


def final_grads_body(
    heads,
    width,
    doc_ref,
    key_ref,
    value_ref,
    near_ref,
    far_ref,
    local_k_ref,
    local_v_ref,
    grad_k_ref,
    grad_v_ref,
):
    piece = key_ref.shape[0]
    states = heads * width
    _, down = label_grids(doc_ref, piece)
    near_label = near_ref[2 * states : 2 * states + LABEL_ROWS, :].astype(F32)[0:1, :]
    far_label = far_ref[2 * states : 2 * states + LABEL_ROWS, :].astype(F32)[0:1, :]
    joined = jnp.broadcast_to((near_label == far_label).astype(F32), (width, width))
    later = ((down + 1).astype(F32)[:, :width] == near_label).astype(F32)

    def state(index):
        rows = slice(index * width, (index + 1) * width)
        return (near_ref[rows, :].astype(F32) + joined * far_ref[rows, :].astype(F32)).astype(BF16)

    for h in range(heads):
        cols = slice(h * width, (h + 1) * width)
        key_h, value_h = key_ref[:, cols], value_ref[:, cols]
        grad_state, gram_grad = state(h), state(heads + h)
        grad_v = local_v_ref[:, cols] + later * mm_nt(key_h, grad_state)
        grad_k = local_k_ref[:, cols] + later * (mm(value_h, grad_state) - mm(key_h, gram_grad))
        grad_v_ref[:, cols] = grad_v.astype(BF16)
        grad_k_ref[:, cols] = grad_k.astype(BF16)


def rotated(value, by):
    devices = lax.axis_size("seq")
    return lax.ppermute(value, "seq", [(i, (i + by) % devices) for i in range(devices)])


def swapped(value, axis, mask):
    devices = lax.axis_size(axis)
    return lax.ppermute(value, axis, [(i, i ^ mask) for i in range(devices)])


def joined_states(near, far, states):
    rows = lax.broadcasted_iota(jnp.int32, near.shape, 0)
    matches = (near[states:, :] == far[states:, :])[0:1, :]
    total = near.astype(F32) + far.astype(F32)
    return jnp.where((rows < states) & matches, total, near.astype(F32)).astype(BF16)


def scan_states(element, states, sign):
    window = lax.axis_size("seq") // 2
    near, far, reach = rotated(element, sign), rotated(element, 2 * sign), 2
    while reach < window:
        near = joined_states(near, far, states)
        far = rotated(near, sign * reach)
        reach *= 2
    return near, far


def per_device(query_rows, key_rows, value_rows, ridge_reg, out_weight, out_grad, doc_ids):
    heads = ridge_reg.shape[0]
    piece, features = key_rows.shape
    width = features // heads
    states = 2 * heads * width
    seq_size, head_size = lax.axis_size("seq"), lax.axis_size("head")
    seq_at, head_at = lax.axis_index("seq"), lax.axis_index("head")
    place = jnp.stack([seq_at, head_at]).astype(jnp.int32)
    model = out_weight.shape[1]
    shard = model // head_size
    doc_row = doc_ids.reshape(1, piece)
    payload = jax.ShapeDtypeStruct((states + LABEL_ROWS, width), BF16)
    rows_bf16 = jax.ShapeDtypeStruct((piece, features), BF16)
    rows_f32 = jax.ShapeDtypeStruct((piece, features), F32)

    (element,) = kernel_call(
        functools.partial(tail_body, heads, width),
        [payload],
        (doc_row, key_rows, value_rows),
        4 * piece * features * width,
        "tail_states",
    )
    near, far = scan_states(element, states, 1)

    cots = [out_grad] + [swapped(out_grad, "head", b) for b in range(1, head_size)]
    out_cot, cot_full = kernel_call(
        functools.partial(cot_body, head_size, shard),
        [rows_bf16, jax.ShapeDtypeStruct((piece, model), BF16)],
        (place, *cots, out_weight),
        2 * piece * features * model,
        "cotangent",
        smem=(0,),
    )

    sol, dual, mixed, back = kernel_call(
        functools.partial(solve_body, heads, width),
        [rows_bf16, rows_bf16, rows_bf16, payload],
        (ridge_reg, doc_row, query_rows, key_rows, value_rows, out_cot, near, far),
        60 * piece * features * width,
        "solve",
        smem=(0,),
    )
    later_near, later_far = scan_states(back, states, -1)

    own, *sends = kernel_call(
        functools.partial(project_body, head_size, shard),
        [jax.ShapeDtypeStruct((piece, shard), F32)]
        + [jax.ShapeDtypeStruct((piece, shard), BF16)] * (head_size - 1),
        (place, mixed, out_weight),
        2 * piece * features * model,
        "project",
        smem=(0,),
    )
    total = own
    for b in range(1, head_size):
        total = total + swapped(sends[b - 1], "head", b).astype(F32)
    layer_out = total.astype(BF16)

    pair_rows = 2 * (model // seq_size)
    pairs = seq_size // 2
    pair_at = seq_at // 2
    cot_blocks, mixed_blocks = [], []
    for c in range(pairs):
        start = jnp.bitwise_xor(pair_at, c) * pair_rows
        block = lax.dynamic_slice_in_dim(cot_full, start, pair_rows, 1)
        cot_blocks.append(block if c == 0 else swapped(block, "seq", 2 * c))
        if c == 0:
            mixed_blocks.append(mixed)
        else:
            low = c & -c
            rest = mixed_blocks[c ^ low]
            mixed_blocks.append(swapped(rest, "seq", 2 * low))
    pair_grad = lax.dot_general(
        jnp.concatenate(cot_blocks, axis=0),
        jnp.concatenate(mixed_blocks, axis=0),
        (((0,), (0,)), ((), ())),
        preferred_element_type=F32,
    )
    halves = pair_grad.reshape(2, pair_rows // 2, features)
    kept = lax.dynamic_index_in_dim(halves, seq_at % 2, 0, False)
    given = lax.dynamic_index_in_dim(halves, 1 - seq_at % 2, 0, False).astype(BF16)
    grad_weight = kept + swapped(given, "seq", 1).astype(F32)

    local_k, local_v = kernel_call(
        functools.partial(local_grads_body, heads, width),
        [rows_f32, rows_f32],
        (doc_row, key_rows, value_rows, out_cot, sol, dual),
        14 * piece * features * width,
        "local_grads",
    )
    grad_keys, grad_values = kernel_call(
        functools.partial(final_grads_body, heads, width),
        [rows_bf16, rows_bf16],
        (doc_row, key_rows, value_rows, later_near, later_far, local_k, local_v),
        6 * piece * features * width,
        "final_grads",
    )
    return (layer_out, dual, grad_keys, grad_values, grad_weight)


def solution(mesh):
    rows = P("seq", "head")
    in_specs = (rows, rows, rows, P("head"), P("head", None), rows, P("seq"))
    return jax.shard_map(
        per_device, mesh=mesh, in_specs=in_specs, out_specs=(rows,) * 5, check_vma=False
    )
```

```python
import functools

import jax
import jax.numpy as jnp
from jax import lax
from jax.experimental import pallas as pl
from jax.experimental.pallas import tpu as pltpu
from jax.sharding import PartitionSpec as P

CG_STEPS = 4
EPSILON = 1e-06
LABEL_ROWS = 16
F32 = jnp.float32
BF16 = jnp.bfloat16
VMEM_LIMIT = 48 * 1024 * 1024
FLOPS_PER_US = 1e9


def mm(a, b):
    return lax.dot_general(a, b, (((1,), (0,)), ((), ())), preferred_element_type=F32)


def mm_nt(a, b):
    return lax.dot_general(a, b, (((1,), (1,)), ((), ())), preferred_element_type=F32)


def mm_tn(a, b):
    return lax.dot_general(a, b, (((0,), (0,)), ((), ())), preferred_element_type=F32)


def kernel_call(body, out_shape, operands, microseconds, name, smem=()):
    in_specs = [
        pl.BlockSpec(memory_space=pltpu.SMEM if i in smem else pltpu.VMEM)
        for i in range(len(operands))
    ]
    nbytes = sum(o.size * o.dtype.itemsize for o in operands)
    nbytes += sum(o.size * o.dtype.itemsize for o in out_shape)
    return pl.pallas_call(
        body,
        out_shape=out_shape,
        in_specs=in_specs,
        out_specs=[pl.BlockSpec(memory_space=pltpu.VMEM)] * len(out_shape),
        compiler_params=pltpu.CompilerParams(vmem_limit_bytes=VMEM_LIMIT),
        cost_estimate=pl.CostEstimate(flops=int(microseconds * FLOPS_PER_US), bytes_accessed=nbytes, transcendentals=0),
        name=name,
    )(*operands)


def label_grids(doc_ref, piece):
    across = jnp.broadcast_to(doc_ref[...], (piece, piece))
    return across, across.T


def document_mask(across, down):
    row = lax.broadcasted_iota(jnp.int32, across.shape, 0)
    col = lax.broadcasted_iota(jnp.int32, across.shape, 1)
    return (across == down) & (col <= row)


def triangle(width):
    row = lax.broadcasted_iota(jnp.int32, (width, width), 0)
    col = lax.broadcasted_iota(jnp.int32, (width, width), 1)
    return col < row, col == row


def pack_symmetric(out_ref, base, extra, matrices):
    width = matrices[0].shape[0]
    below, diagonal = triangle(width)
    rows = []
    for pair in range(len(matrices) // 2):
        one, two = matrices[2 * pair], matrices[2 * pair + 1]
        square = jnp.where(below | diagonal, one, two)
        out_ref[base + pair * width : base + (pair + 1) * width, :] = square.astype(BF16)
        rows.append(jnp.sum(jnp.where(diagonal, two, 0.0), axis=0, keepdims=True))
    rows.append(jnp.broadcast_to(extra, (LABEL_ROWS - len(rows), width)))
    out_ref[base + len(matrices) // 2 * width :, :] = jnp.concatenate(rows, axis=0).astype(BF16)


def unpack_symmetric(square, row):
    below, diagonal = triangle(square.shape[0])
    flipped = square.T
    one = jnp.where(below | diagonal, square, flipped)
    two = jnp.where(diagonal, row, jnp.where(below, flipped, square))
    return one, two


def received_states(near_ref, far_ref, heads, width):
    base = heads * width
    tail = base + heads // 2 * width
    near_rest = near_ref[tail : tail + LABEL_ROWS, :].astype(F32)
    far_rest = far_ref[tail : tail + LABEL_ROWS, :].astype(F32)
    label = near_rest[LABEL_ROWS - 1 :, :]
    joined = (label == far_rest[LABEL_ROWS - 1 :, :]).astype(F32)
    rest = near_rest + joined * far_rest

    def square(index):
        rows = slice(index * width, (index + 1) * width)
        return near_ref[rows, :].astype(F32) + joined * far_ref[rows, :].astype(F32)

    full = [square(h).astype(BF16) for h in range(heads)]
    symmetric = []
    for pair in range(heads // 2):
        for matrix in unpack_symmetric(square(heads + pair), rest[pair : pair + 1, :]):
            symmetric.append(matrix.astype(BF16))
    return label, full, symmetric


def tail_body(heads, width, doc_ref, key_ref, value_ref, out_ref):
    piece = key_ref.shape[0]
    across, down = label_grids(doc_ref, piece)
    last = jnp.max(across, axis=1, keepdims=True)
    tail = (down == last).astype(F32).astype(BF16)
    grams = []
    for h in range(heads):
        cols = slice(h * width, (h + 1) * width)
        key_h = key_ref[:, cols]
        masked = key_h * tail[:, :width]
        grams.append(mm_tn(key_h, masked))
        out_ref[h * width : (h + 1) * width, :] = mm_tn(value_ref[:, cols], masked).astype(BF16)
    pack_symmetric(out_ref, heads * width, (last[:1] + 1).astype(F32), grams)


def cot_body(count, shard, place_ref, *refs):
    cots, weight_ref, cot_ref, full_ref = refs[:count], refs[count], refs[count + 1], refs[count + 2]
    me = place_ref[1]
    total = None
    for b in range(count):
        owner = jnp.bitwise_xor(me, b)
        cols = pl.ds(pl.multiple_of(owner * shard, shard), shard)
        block = cots[b][...]
        full_ref[:, cols] = block
        part = mm_nt(block, weight_ref[:, cols])
        total = part if total is None else total + part
    cot_ref[...] = total.astype(BF16)


def project_body(count, shard, place_ref, mixed_ref, weight_ref, own_ref, *send_refs):
    me = place_ref[1]
    mixed = mixed_ref[...]
    for b in range(count):
        owner = jnp.bitwise_xor(me, b)
        cols = pl.ds(pl.multiple_of(owner * shard, shard), shard)
        part = mm(mixed, weight_ref[:, cols])
        if b == 0:
            own_ref[...] = part
        else:
            send_refs[b - 1][...] = part.astype(BF16)


def solve_body(
    heads,
    width,
    ridge_ref,
    doc_ref,
    query_ref,
    key_ref,
    value_ref,
    cot_ref,
    near_ref,
    far_ref,
    sol_ref,
    dual_ref,
    mixed_ref,
    out_ref,
):
    piece = key_ref.shape[0]
    across, down = label_grids(doc_ref, piece)
    same = document_mask(across, down).astype(F32)
    same_two = jnp.concatenate([same, same], axis=0)
    first = jnp.min(across, axis=1, keepdims=True)
    head_rows = (down == first)[:, :width].astype(F32)
    label, value_states, gram_states = received_states(near_ref, far_ref, heads, width)
    carried = ((down + 1).astype(F32)[:, :width] == label).astype(F32)
    carried_two = jnp.concatenate([carried, carried], axis=0)
    keys, rhs_keys, values, solutions, residuals, directions, squares = ([] for _ in range(7))
    for h in range(heads):
        cols = slice(h * width, (h + 1) * width)
        key_h = key_ref[:, cols]
        value_h = value_ref[:, cols]
        cot_h = cot_ref[:, cols]
        both = mm(cot_h, jnp.concatenate([value_h.T, value_states[h]], axis=1))
        scores = (both[:, :piece] * same).astype(BF16)
        target = carried * both[:, piece:] + mm(scores, key_h)
        start = jnp.concatenate([query_ref[:, cols].astype(F32), target], axis=0)
        keys.append(key_h)
        values.append(value_h)
        rhs_keys.append(jnp.concatenate([key_h.T, gram_states[h]], axis=1))
        solutions.append(jnp.zeros_like(start))
        residuals.append(start)
        directions.append(start)
        squares.append(jnp.sum(start * start, axis=1, keepdims=True))
    for step in range(CG_STEPS):
        for h in range(heads):
            p = directions[h]
            both = mm(p.astype(BF16), rhs_keys[h])
            scores = (both[:, :piece] * same_two).astype(BF16)
            applied = carried_two * both[:, piece:] + mm(scores, keys[h]) + ridge_ref[h] * p
            size = squares[h] / (jnp.sum(p * applied, axis=1, keepdims=True) + EPSILON)
            solutions[h] = solutions[h] + size * p
            if step + 1 < CG_STEPS:
                residuals[h] = residuals[h] - size * applied
                new_sq = jnp.sum(residuals[h] * residuals[h], axis=1, keepdims=True)
                directions[h] = residuals[h] + new_sq / (squares[h] + EPSILON) * p
                squares[h] = new_sq
    crosses = []
    for h in range(heads):
        cols = slice(h * width, (h + 1) * width)
        sol = solutions[h][:piece]
        sol_b = sol.astype(BF16)
        dual_b = solutions[h][piece:].astype(BF16)
        both = mm(sol_b, jnp.concatenate([rhs_keys[h][:, :piece], value_states[h].T], axis=1))
        scores = (both[:, :piece] * same).astype(BF16)
        output = carried * both[:, piece:] + mm(scores, values[h])
        mixed_ref[:, cols] = output.astype(BF16)
        sol_ref[:, cols] = sol_b
        dual_ref[:, cols] = dual_b
        masked = (head_rows * sol).astype(BF16)
        out_ref[h * width : (h + 1) * width, :] = mm_tn(cot_ref[:, cols], masked).astype(BF16)
        cross = mm_tn(dual_b, masked)
        crosses.append(cross + cross.T)
    pack_symmetric(out_ref, heads * width, (first[:1] + 1).astype(F32), crosses)


def local_grads_body(
    heads, width, doc_ref, key_ref, value_ref, cot_ref, sol_ref, dual_ref, grad_k_ref, grad_v_ref
):
    piece = key_ref.shape[0]
    across, down = label_grids(doc_ref, piece)
    same = document_mask(across, down).astype(F32)
    same_two = jnp.concatenate([same, same], axis=0)
    for h in range(heads):
        cols = slice(h * width, (h + 1) * width)
        key_h, value_h, cot_h = key_ref[:, cols], value_ref[:, cols], cot_ref[:, cols]
        sol, dual = sol_ref[:, cols], dual_ref[:, cols]
        score_two = (mm_nt(cot_h, value_h) * same).astype(BF16)
        pair = (mm_nt(jnp.concatenate([sol, dual], axis=0), key_h) * same_two).astype(BF16)
        score_one, score_three = pair[:piece], pair[piece:]
        grad_v_ref[:, cols] = mm_tn(score_one, cot_h)
        grad_k_ref[:, cols] = mm_tn(
            jnp.concatenate([score_two, -score_three, -score_one], axis=0),
            jnp.concatenate([sol, sol, dual], axis=0),
        )


def final_grads_body(
    heads,
    width,
    doc_ref,
    key_ref,
    value_ref,
    near_ref,
    far_ref,
    local_k_ref,
    local_v_ref,
    grad_k_ref,
    grad_v_ref,
):
    piece = key_ref.shape[0]
    _, down = label_grids(doc_ref, piece)
    label, grad_states, gram_grads = received_states(near_ref, far_ref, heads, width)
    later = ((down + 1).astype(F32)[:, :width] == label).astype(F32)
    for h in range(heads):
        cols = slice(h * width, (h + 1) * width)
        key_h, value_h = key_ref[:, cols], value_ref[:, cols]
        grad_state, gram_grad = grad_states[h], gram_grads[h]
        grad_v = local_v_ref[:, cols] + later * mm_nt(key_h, grad_state)
        grad_k = local_k_ref[:, cols] + later * (mm(value_h, grad_state) - mm(key_h, gram_grad))
        grad_v_ref[:, cols] = grad_v.astype(BF16)
        grad_k_ref[:, cols] = grad_k.astype(BF16)


def rotated(value, by):
    devices = lax.axis_size("seq")
    return lax.ppermute(value, "seq", [(i, (i + by) % devices) for i in range(devices)])


def swapped(value, axis, mask):
    devices = lax.axis_size(axis)
    return lax.ppermute(value, axis, [(i, i ^ mask) for i in range(devices)])


def joined_states(near, far):
    rows = lax.broadcasted_iota(jnp.int32, near.shape, 0)
    numbers = near.shape[0] - LABEL_ROWS // 2
    matches = (near[-1:, :] == far[-1:, :]) & (rows < numbers)
    total = near.astype(F32) + far.astype(F32)
    return jnp.where(matches, total, near.astype(F32)).astype(BF16)


def scan_states(element, sign, beside):
    window = lax.axis_size("seq") // 2
    near, far, reach = rotated(element, sign), rotated(element, 2 * sign), 2
    near, far, beside = lax.optimization_barrier((near, far, beside))
    while reach < window:
        near = joined_states(near, far)
        far = rotated(near, sign * reach)
        reach *= 2
    return near, far, beside


def per_device(query_rows, key_rows, value_rows, ridge_reg, out_weight, out_grad, doc_ids):
    heads = ridge_reg.shape[0]
    piece, features = key_rows.shape
    width = features // heads
    states = heads * width + heads // 2 * width
    seq_size, head_size = lax.axis_size("seq"), lax.axis_size("head")
    seq_at, head_at = lax.axis_index("seq"), lax.axis_index("head")
    place = jnp.stack([seq_at, head_at]).astype(jnp.int32)
    model = out_weight.shape[1]
    shard = model // head_size
    doc_row = doc_ids.reshape(1, piece)
    payload = jax.ShapeDtypeStruct((states + LABEL_ROWS, width), BF16)
    rows_bf16 = jax.ShapeDtypeStruct((piece, features), BF16)
    rows_f32 = jax.ShapeDtypeStruct((piece, features), F32)

    (element,) = kernel_call(
        functools.partial(tail_body, heads, width),
        [payload],
        (doc_row, key_rows, value_rows),
        0.5,
        "tail_states",
    )
    cots = [out_grad] + [swapped(out_grad, "head", b) for b in range(1, head_size)]
    near, far, cots = scan_states(element, 1, cots)
    out_cot, cot_full = kernel_call(
        functools.partial(cot_body, head_size, shard),
        [rows_bf16, jax.ShapeDtypeStruct((piece, model), BF16)],
        (place, *cots, out_weight),
        1.5,
        "cotangent",
        smem=(0,),
    )

    sol, dual, mixed, back = kernel_call(
        functools.partial(solve_body, heads, width),
        [rows_bf16, rows_bf16, rows_bf16, payload],
        (ridge_reg, doc_row, query_rows, key_rows, value_rows, out_cot, near, far),
        5.0,
        "solve",
        smem=(0,),
    )
    own, *sends = kernel_call(
        functools.partial(project_body, head_size, shard),
        [jax.ShapeDtypeStruct((piece, shard), F32)]
        + [jax.ShapeDtypeStruct((piece, shard), BF16)] * (head_size - 1),
        (place, mixed, out_weight),
        1.0,
        "project",
        smem=(0,),
    )
    total = own
    for b in range(1, head_size):
        total = total + swapped(sends[b - 1], "head", b).astype(F32)
    layer_out = total.astype(BF16)

    pair_rows = 2 * (model // seq_size)
    pairs = seq_size // 2
    pair_at = seq_at // 2
    cot_blocks = []
    for c in range(pairs):
        start = jnp.bitwise_xor(pair_at, c) * pair_rows
        block = lax.dynamic_slice_in_dim(cot_full, start, pair_rows, 1)
        cot_blocks.append(block if c == 0 else swapped(block, "seq", 2 * c))
    gathered, cot_blocks = lax.optimization_barrier((mixed, cot_blocks))
    mixed_blocks = [gathered] + [None] * (pairs - 1)
    for c in range(1, pairs):
        if c & (c - 1) == 0:
            mixed_blocks[c] = swapped(gathered, "seq", 2 * c)
    later_near, later_far, mixed_blocks = scan_states(back, -1, mixed_blocks)
    for c in range(1, pairs):
        low = c & -c
        if c != low:
            mixed_blocks[c] = swapped(mixed_blocks[c ^ low], "seq", 2 * low)
    pair_grad = lax.dot_general(
        jnp.concatenate(cot_blocks, axis=0),
        jnp.concatenate(mixed_blocks, axis=0),
        (((0,), (0,)), ((), ())),
        preferred_element_type=F32,
    )
    halves = pair_grad.reshape(2, pair_rows // 2, features)
    kept = lax.dynamic_index_in_dim(halves, seq_at % 2, 0, False)
    given = lax.dynamic_index_in_dim(halves, 1 - seq_at % 2, 0, False).astype(BF16)
    grad_weight = kept + swapped(given, "seq", 1).astype(F32)

    local_k, local_v = kernel_call(
        functools.partial(local_grads_body, heads, width),
        [rows_f32, rows_f32],
        (doc_row, key_rows, value_rows, out_cot, sol, dual),
        1.1,
        "local_grads",
    )
    grad_keys, grad_values = kernel_call(
        functools.partial(final_grads_body, heads, width),
        [rows_bf16, rows_bf16],
        (doc_row, key_rows, value_rows, later_near, later_far, local_k, local_v),
        1.0,
        "final_grads",
    )
    return (layer_out, dual, grad_keys, grad_values, grad_weight)


def solution(mesh):
    rows = P("seq", "head")
    in_specs = (rows, rows, rows, P("head"), P("head", None), rows, P("seq"))
    return jax.shard_map(
        per_device, mesh=mesh, in_specs=in_specs, out_specs=(rows,) * 5, check_vma=False
    )
```

```python
import functools

import jax
import jax.numpy as jnp
from jax import lax
from jax.experimental import pallas as pl
from jax.experimental.pallas import tpu as pltpu
from jax.sharding import PartitionSpec as P

CG_STEPS = 4
EPSILON = 1e-06
LABEL_ROWS = 16
F32 = jnp.float32
BF16 = jnp.bfloat16
VMEM_LIMIT = 48 * 1024 * 1024
FLOPS_PER_US = 1e9
COT_US = 1.5
FINAL_US = 1.0
PAIR_JOIN_US = 5.0
MINE_US = 6.0


def mm(a, b):
    return lax.dot_general(a, b, (((1,), (0,)), ((), ())), preferred_element_type=F32)


def mm_nt(a, b):
    return lax.dot_general(a, b, (((1,), (1,)), ((), ())), preferred_element_type=F32)


def mm_tn(a, b):
    return lax.dot_general(a, b, (((0,), (0,)), ((), ())), preferred_element_type=F32)


def kernel_call(body, out_shape, operands, microseconds, name, smem=(), scratch=()):
    nbytes = sum(o.size * o.dtype.itemsize for o in operands)
    nbytes += sum(o.size * o.dtype.itemsize for o in out_shape)
    return pl.pallas_call(
        body,
        out_shape=out_shape,
        in_specs=[
            pl.BlockSpec(memory_space=pltpu.SMEM if i in smem else pltpu.VMEM)
            for i in range(len(operands))
        ],
        out_specs=[pl.BlockSpec(memory_space=pltpu.VMEM)] * len(out_shape),
        scratch_shapes=scratch,
        compiler_params=pltpu.CompilerParams(vmem_limit_bytes=VMEM_LIMIT),
        cost_estimate=pl.CostEstimate(
            flops=int(microseconds * FLOPS_PER_US), bytes_accessed=nbytes, transcendentals=0
        ),
        name=name,
    )(*operands)


def label_grids(rows_ref):
    piece = rows_ref.shape[0] - LABEL_ROWS
    labels = rows_ref[piece : piece + LABEL_ROWS, :piece].astype(F32)[0:1, :]
    across = jnp.broadcast_to(labels, (piece, piece))
    return piece, across, across.T


def document_mask(across, down):
    row = lax.broadcasted_iota(jnp.int32, across.shape, 0)
    col = lax.broadcasted_iota(jnp.int32, across.shape, 1)
    return (across == down) & (col <= row)


def triangle(width):
    row = lax.broadcasted_iota(jnp.int32, (width, width), 0)
    col = lax.broadcasted_iota(jnp.int32, (width, width), 1)
    return col < row, col == row


def unit_rows(width):
    return 3 * width + LABEL_ROWS


def pack_states(out_ref, label, full, symmetric):
    width = full[0].shape[0]
    below, diagonal = triangle(width)
    for unit in range(len(full) // 2):
        base = unit * unit_rows(width)
        for i in range(2):
            rows = slice(base + i * width, base + (i + 1) * width)
            out_ref[rows, :] = full[2 * unit + i].astype(BF16)
        one, two = symmetric[2 * unit], symmetric[2 * unit + 1]
        square = jnp.where(below | diagonal, one, two)
        out_ref[base + 2 * width : base + 3 * width, :] = square.astype(BF16)
        second = jnp.sum(jnp.where(diagonal, two, 0.0), axis=0, keepdims=True)
        rest = jnp.broadcast_to(label, (LABEL_ROWS - 1, width))
        out_ref[base + 3 * width : base + unit_rows(width), :] = jnp.concatenate(
            [second, rest], axis=0
        ).astype(BF16)


def join_units(near, far, width):
    total = near.astype(F32)
    tail = slice(near.shape[0] - LABEL_ROWS, near.shape[0])
    near_label, far_label = near[tail].astype(F32), far[tail].astype(F32)
    joined = (near_label[LABEL_ROWS - 1 :] == far_label[LABEL_ROWS - 1 :]).astype(F32)
    total = total + joined * far.astype(F32)
    row = lax.rem(lax.broadcasted_iota(jnp.int32, near.shape, 0), unit_rows(width))
    return jnp.where(row <= 3 * width, total, near.astype(F32))


def unpack_symmetric(square, row):
    below, diagonal = triangle(square.shape[0])
    flipped = square.T
    one = jnp.where(below | diagonal, square, flipped)
    two = jnp.where(diagonal, row, jnp.where(below, flipped, square))
    return one, two


def unpack_states(units, heads, width):
    size = unit_rows(width)
    label = units[size - 1 : size, :]
    full, symmetric = [], []
    for unit in range(heads // 2):
        part = units[unit * size : (unit + 1) * size, :]
        full += [part[:width].astype(BF16), part[width : 2 * width].astype(BF16)]
        square = part[2 * width : 3 * width]
        symmetric += [
            m.astype(BF16) for m in unpack_symmetric(square, part[3 * width : 3 * width + 1])
        ]
    return label, full, symmetric


def head_rows_of(rows_ref, heads, width, part, h):
    start = (part * heads + h) * width
    return rows_ref[: rows_ref.shape[0] - LABEL_ROWS, start : start + width]


def tail_body(heads, width, rows_ref, out_ref):
    piece, across, down = label_grids(rows_ref)
    last = jnp.max(across, axis=1, keepdims=True)
    tail = (down == last).astype(F32).astype(BF16)
    sums, grams = [], []
    for h in range(heads):
        key_h = head_rows_of(rows_ref, heads, width, 0, h)
        value_h = head_rows_of(rows_ref, heads, width, 1, h)
        masked = key_h * tail[:, :width]
        grams.append(mm_tn(key_h, masked))
        sums.append(mm_tn(value_h, masked))
    pack_states(out_ref, last[:1] + 1, sums, grams)


def cot_body(count, shard, place_ref, *refs):
    cots, weight_ref, cot_ref = refs[:count], refs[count], refs[count + 1]
    me = place_ref[1]
    total = None
    for b in range(count):
        owner = jnp.bitwise_xor(me, b)
        cols = pl.ds(pl.multiple_of(owner * shard, shard), shard)
        part = mm_nt(cots[b][...], weight_ref[:, cols])
        total = part if total is None else total + part
    cot_ref[...] = total.astype(BF16)


def project_body(count, shard, place_ref, mixed_ref, weight_ref, turned_ref, keep_ref, send_ref):
    piece = mixed_ref.shape[0]
    me = place_ref[1]
    mixed = mixed_ref[...]
    for c in range(count):
        owner = jnp.bitwise_xor(me, c)
        cols = pl.ds(pl.multiple_of(owner * shard, shard), shard)
        part = mm(mixed, weight_ref[:, cols])
        rows = slice(c // 2 * piece, (c // 2 + 1) * piece)
        if c % 2:
            send_ref[rows, :] = part.astype(BF16)
        else:
            keep_ref[rows, :] = part
    send_ref[count // 2 * piece :, :] = turned_ref[...]


def halve_body(blocks, piece, keep_ref, got_ref, turned_ref, rest_ref, send_ref):
    for c in range(blocks):
        rows = slice(c * piece, (c + 1) * piece)
        target = slice(c // 2 * piece, (c // 2 + 1) * piece)
        total = keep_ref[rows, :] + got_ref[rows, :].astype(F32)
        if c % 2:
            send_ref[target, :] = total.astype(BF16)
        else:
            rest_ref[target, :] = total
    sent, gathered = blocks // 2 * piece, turned_ref.shape[0]
    send_ref[sent : sent + gathered, :] = turned_ref[...]
    send_ref[sent + gathered :, :] = got_ref[blocks * piece :, :]


def join_body(width, near_ref, far_ref, *refs):
    out_ref = refs[-1]
    out_ref[...] = join_units(near_ref[...], far_ref[...], width).astype(BF16)


def pair_join_body(width, place_ref, here_ref, there_ref, out_ref, both_ref):
    half = out_ref.shape[0]
    odd = lax.rem(place_ref[0], 2)
    mine = pl.ds(pl.multiple_of(odd * half, LABEL_ROWS), half)
    both_ref[pl.ds(pl.multiple_of(odd * half, LABEL_ROWS), half), :] = here_ref[mine, :]
    both_ref[pl.ds(pl.multiple_of((1 - odd) * half, LABEL_ROWS), half), :] = there_ref[mine, :]
    total = join_units(both_ref[:half, :], both_ref[half:, :], width)
    out_ref[...] = total.astype(BF16)


def pair_grad_body(piece, parts, arrays, by_place, place_ref, *refs):
    count = len(parts)
    cots, mixes = refs[:arrays], refs[arrays : arrays + count]
    kept_ref, given_ref, cot_ref, mix_ref, total_ref = refs[arrays + count :]
    for i, (array, row) in enumerate(parts):
        cot_at = jnp.bitwise_xor(place_ref[1], i) if by_place else i
        mix_at = jnp.bitwise_xor(lax.div(place_ref[0], 2), i) if by_place else i
        cot = cots[array][row : row + piece, :]
        cot_ref[pl.ds(pl.multiple_of(cot_at * piece, piece), piece), :] = cot
        mix_ref[pl.ds(pl.multiple_of(mix_at * piece, piece), piece), :] = mixes[i][...]
    total_ref[...] = mm_tn(cot_ref[...], mix_ref[...])
    half = kept_ref.shape[0]
    odd = lax.rem(place_ref[0], 2)
    kept_ref[...] = total_ref[pl.ds(pl.multiple_of(odd * half, half), half), :]
    given_ref[...] = total_ref[pl.ds(pl.multiple_of((1 - odd) * half, half), half), :].astype(BF16)


def solve_body(
    heads,
    width,
    ridge_ref,
    rows_ref,
    cot_ref,
    near_ref,
    far_ref,
    sol_ref,
    dual_ref,
    mixed_ref,
    out_ref,
):
    piece, across, down = label_grids(rows_ref)
    same = document_mask(across, down).astype(F32)
    same_two = jnp.concatenate([same, same], axis=0)
    first = jnp.min(across, axis=1, keepdims=True)
    head_rows = (down == first)[:, :width].astype(F32)
    units = join_units(near_ref[...], far_ref[...], width)
    label, value_states, gram_states = unpack_states(units, heads, width)
    carried = ((down + 1)[:, :width] == label).astype(F32)
    carried_two = jnp.concatenate([carried, carried], axis=0)
    keys, rhs_keys, values, solutions, residuals, directions, squares = ([] for _ in range(7))
    for h in range(heads):
        cols = slice(h * width, (h + 1) * width)
        key_h = head_rows_of(rows_ref, heads, width, 0, h)
        value_h = head_rows_of(rows_ref, heads, width, 1, h)
        query_h = head_rows_of(rows_ref, heads, width, 2, h)
        cot_h = cot_ref[:, cols]
        both = mm(cot_h, jnp.concatenate([value_h.T, value_states[h]], axis=1))
        scores = (both[:, :piece] * same).astype(BF16)
        target = carried * both[:, piece:] + mm(scores, key_h)
        start = jnp.concatenate([query_h.astype(F32), target], axis=0)
        keys.append(key_h)
        values.append(value_h)
        rhs_keys.append(jnp.concatenate([key_h.T, gram_states[h]], axis=1))
        solutions.append(jnp.zeros_like(start))
        residuals.append(start)
        directions.append(start)
        squares.append(jnp.sum(start * start, axis=1, keepdims=True))
    for step in range(CG_STEPS):
        for h in range(heads):
            p = directions[h]
            both = mm(p.astype(BF16), rhs_keys[h])
            scores = (both[:, :piece] * same_two).astype(BF16)
            applied = carried_two * both[:, piece:] + mm(scores, keys[h]) + ridge_ref[h] * p
            size = squares[h] / (jnp.sum(p * applied, axis=1, keepdims=True) + EPSILON)
            solutions[h] = solutions[h] + size * p
            if step + 1 < CG_STEPS:
                residuals[h] = residuals[h] - size * applied
                new_sq = jnp.sum(residuals[h] * residuals[h], axis=1, keepdims=True)
                directions[h] = residuals[h] + new_sq / (squares[h] + EPSILON) * p
                squares[h] = new_sq
    sums, crosses = [], []
    for h in range(heads):
        cols = slice(h * width, (h + 1) * width)
        sol = solutions[h][:piece]
        sol_b = sol.astype(BF16)
        dual_b = solutions[h][piece:].astype(BF16)
        both = mm(sol_b, jnp.concatenate([rhs_keys[h][:, :piece], value_states[h].T], axis=1))
        scores = (both[:, :piece] * same).astype(BF16)
        output = carried * both[:, piece:] + mm(scores, values[h])
        mixed_ref[:, cols] = output.astype(BF16)
        sol_ref[:, cols] = sol_b
        dual_ref[:, cols] = dual_b
        masked = (head_rows * sol).astype(BF16)
        sums.append(mm_tn(cot_ref[:, cols], masked))
        cross = mm_tn(dual_b, masked)
        crosses.append(cross + cross.T)
    pack_states(out_ref, first[:1] + 1, sums, crosses)


def local_grads_body(
    heads, width, rows_ref, cot_ref, sol_ref, dual_ref, grad_k_ref, grad_v_ref
):
    piece, across, down = label_grids(rows_ref)
    same = document_mask(across, down).astype(F32)
    same_two = jnp.concatenate([same, same], axis=0)
    for h in range(heads):
        cols = slice(h * width, (h + 1) * width)
        key_h = head_rows_of(rows_ref, heads, width, 0, h)
        value_h = head_rows_of(rows_ref, heads, width, 1, h)
        cot_h = cot_ref[:, cols]
        sol, dual = sol_ref[:, cols], dual_ref[:, cols]
        score_two = (mm_nt(cot_h, value_h) * same).astype(BF16)
        pair = (mm_nt(jnp.concatenate([sol, dual], axis=0), key_h) * same_two).astype(BF16)
        score_one, score_three = pair[:piece], pair[piece:]
        grad_v_ref[:, cols] = mm_tn(score_one, cot_h)
        grad_k_ref[:, cols] = mm_tn(
            jnp.concatenate([score_two, -score_three, -score_one], axis=0),
            jnp.concatenate([sol, sol, dual], axis=0),
        )


def final_grads_body(
    heads,
    width,
    place_ref,
    rows_ref,
    there_ref,
    mine_ref,
    theirs_ref,
    local_k_ref,
    local_v_ref,
    grad_k_ref,
    grad_v_ref,
    later_ref,
):
    piece, _, down = label_grids(rows_ref)
    half = mine_ref.shape[0]
    odd = lax.rem(place_ref[0], 2)
    later_ref[pl.ds(pl.multiple_of(odd * half, LABEL_ROWS), half), :] = mine_ref[...]
    later_ref[pl.ds(pl.multiple_of((1 - odd) * half, LABEL_ROWS), half), :] = theirs_ref[...]
    units = jnp.where(
        odd == 1,
        later_ref[...].astype(F32),
        join_units(there_ref[...], later_ref[...], width),
    )
    label, grad_states, gram_grads = unpack_states(units, heads, width)
    later = ((down + 1)[:, :width] == label).astype(F32)
    for h in range(heads):
        cols = slice(h * width, (h + 1) * width)
        key_h = head_rows_of(rows_ref, heads, width, 0, h)
        value_h = head_rows_of(rows_ref, heads, width, 1, h)
        grad_state, gram_grad = grad_states[h], gram_grads[h]
        grad_v = local_v_ref[:, cols] + later * mm_nt(key_h, grad_state)
        grad_k = local_k_ref[:, cols] + later * (mm(value_h, grad_state) - mm(key_h, gram_grad))
        grad_v_ref[:, cols] = grad_v.astype(BF16)
        grad_k_ref[:, cols] = grad_k.astype(BF16)


def rotated(value, by):
    devices = lax.axis_size("seq")
    return lax.ppermute(value, "seq", [(i, (i + by) % devices) for i in range(devices)])


def swapped(value, axis, mask):
    devices = lax.axis_size(axis)
    return lax.ppermute(value, axis, [(i, i ^ mask) for i in range(devices)])


def joined_inputs(key_rows, value_rows, query_rows, doc_row):
    piece, features = key_rows.shape
    parts = (key_rows, value_rows, query_rows)
    width = len(parts) * features
    total = jnp.pad(
        doc_row.astype(BF16), ((piece, LABEL_ROWS - 1), (0, width - doc_row.shape[1]))
    )
    for i, part in enumerate(parts):
        total += jnp.pad(part, ((0, LABEL_ROWS), (i * features, width - (i + 1) * features)))
    return total


def join_states(near, far, width, *after):
    (joined,) = kernel_call(
        functools.partial(join_body, width),
        [jax.ShapeDtypeStruct(far.shape, BF16)],
        (near, far, *after),
        MINE_US if after else 0.5,
        "join_states",
    )
    return joined


def per_device(query_rows, key_rows, value_rows, ridge_reg, out_weight, out_grad, doc_ids):
    heads = ridge_reg.shape[0]
    piece, features = key_rows.shape
    width = features // heads
    seq_size, head_size = lax.axis_size("seq"), lax.axis_size("head")
    seq_at, head_at = lax.axis_index("seq"), lax.axis_index("head")
    place = jnp.stack([seq_at, head_at]).astype(jnp.int32)
    model = out_weight.shape[1]
    shard = model // head_size
    doc_row = doc_ids.reshape(1, piece)
    payload = jax.ShapeDtypeStruct((heads // 2 * unit_rows(width), width), BF16)
    half_payload = jax.ShapeDtypeStruct((payload.shape[0] // 2, width), BF16)
    rows_bf16 = jax.ShapeDtypeStruct((piece, features), BF16)
    rows_f32 = jax.ShapeDtypeStruct((piece, features), F32)
    window = seq_size // 2
    pairs = seq_size // 2
    pair_rows = model // pairs
    pair_at = seq_at // 2
    square = pairs == head_size

    rows_in = joined_inputs(key_rows, value_rows, query_rows, doc_row)
    (element,) = kernel_call(
        functools.partial(tail_body, heads, width),
        [payload],
        (rows_in,),
        0.5,
        "tail_states",
    )
    near, far, reach = rotated(element, 1), rotated(element, 2), 2
    cots = [out_grad] + [swapped(out_grad, "head", b) for b in range(1, head_size)]
    near, far, cots = lax.optimization_barrier((near, far, cots))
    while reach < window:
        near = join_states(near, far, width)
        far = rotated(near, reach)
        reach *= 2
    near, cot_here = lax.optimization_barrier((near, out_grad))
    if square:
        turned = lax.ppermute(
            cot_here,
            ("seq", "head"),
            [
                ((2 * z + y) * head_size + h, (2 * h + y) * head_size + z)
                for z in range(pairs)
                for y in range(2)
                for h in range(head_size)
            ],
        )
    else:
        turned = cot_here

    (out_cot,) = kernel_call(
        functools.partial(cot_body, head_size, shard),
        [rows_bf16],
        (place, *cots, out_weight),
        1.5,
        "cotangent",
        smem=(0,),
    )
    sol, dual, mixed, back = kernel_call(
        functools.partial(solve_body, heads, width),
        [rows_bf16, rows_bf16, rows_bf16, payload],
        (ridge_reg, rows_in, out_cot, near, far),
        5.0,
        "solve",
        smem=(0,),
    )
    mixes = [mixed] + [None] * (pairs - 1)
    for step in range(1, pairs):
        if not square:
            mixes[step] = rotated(mixed, -2 * step)
        elif step & (step - 1) == 0:
            mixes[step] = swapped(mixed, "seq", 2 * step)
    there = swapped(back, "seq", 1)
    (pair_half,) = kernel_call(
        functools.partial(pair_join_body, width),
        [half_payload],
        (place, back, there),
        PAIR_JOIN_US,
        "pair_join",
        smem=(0,),
        scratch=[pltpu.VMEM(payload.shape, BF16)],
    )
    ready, turned = lax.optimization_barrier((mixed, turned))
    blocks = head_size // 2
    keep, send = kernel_call(
        functools.partial(project_body, head_size, shard),
        [
            jax.ShapeDtypeStruct((blocks * piece, shard), F32),
            jax.ShapeDtypeStruct((blocks * piece + piece, shard), BF16),
        ],
        (place, ready, out_weight, turned),
        1.0,
        "project",
        smem=(0,),
    )
    gathered, parts = [turned], [(0, 0)]
    mask, so_far = 1, turned
    got = swapped(send, "head", mask)
    held = {i: mixes[i] for i in range(1, pairs) if mixes[i] is not None and i % 2 == 0}
    held, got, after = lax.optimization_barrier((held, got, pair_half))
    near, far, reach = rotated(pair_half, -2), rotated(pair_half, -4), 4
    while reach < window:
        near = join_states(near, far, width)
        far = rotated(near, -reach)
        reach *= 2
    mine = join_states(near, far, width, after)
    theirs = swapped(mine, "seq", 1)
    for step in range(1, pairs):
        low = step & -step
        if mixes[step] is None:
            held[step] = mixes[step] = swapped(held[step ^ low], "seq", 2 * low)

    while blocks > 1:
        for c in range(mask):
            parts.append((len(gathered), (blocks + c) * piece))
        gathered.append(got)
        blocks //= 2
        mask *= 2
        keep, send = kernel_call(
            functools.partial(halve_body, 2 * blocks, piece),
            [
                jax.ShapeDtypeStruct((blocks * piece, shard), F32),
                jax.ShapeDtypeStruct((blocks * piece + mask * piece, shard), BF16),
            ],
            (keep, got, so_far),
            0.5,
            "halve",
        )
        so_far = send[blocks * piece :]
        got = swapped(send, "head", mask)
    for c in range(mask):
        parts.append((len(gathered), (blocks + c) * piece))
    gathered.append(got)
    layer_out = (keep + got[:piece].astype(F32)).astype(BF16)
    if not square:
        cot_full = lax.all_gather(out_grad, "head", axis=1, tiled=True)
        gathered = []
        for step in range(pairs):
            start = lax.rem(pair_at + pairs - step, pairs) * pair_rows
            block = lax.dynamic_slice_in_dim(cot_full, start, pair_rows, 1)
            gathered.append(rotated(block, -2 * step) if step else block)
        parts = [(step, 0) for step in range(pairs)]

    kept, given = kernel_call(
        functools.partial(pair_grad_body, piece, tuple(parts), len(gathered), square),
        [
            jax.ShapeDtypeStruct((pair_rows // 2, features), F32),
            jax.ShapeDtypeStruct((pair_rows // 2, features), BF16),
        ],
        (place, *gathered, *mixes),
        1.5,
        "pair_grad",
        smem=(0,),
        scratch=[
            pltpu.VMEM((pairs * piece, pair_rows), BF16),
            pltpu.VMEM((pairs * piece, features), BF16),
            pltpu.VMEM((pair_rows, features), F32),
        ],
    )
    grad_weight = kept + swapped(given, "seq", 1).astype(F32)

    local_k, local_v = kernel_call(
        functools.partial(local_grads_body, heads, width),
        [rows_f32, rows_f32],
        (rows_in, out_cot, sol, dual),
        1.1,
        "local_grads",
    )
    grad_keys, grad_values = kernel_call(
        functools.partial(final_grads_body, heads, width),
        [rows_bf16, rows_bf16],
        (place, rows_in, there, mine, theirs, local_k, local_v),
        FINAL_US,
        "final_grads",
        smem=(0,),
        scratch=[pltpu.VMEM(payload.shape, BF16)],
    )
    return (layer_out, dual, grad_keys, grad_values, grad_weight)


def solution(mesh):
    rows = P("seq", "head")
    in_specs = (rows, rows, rows, P("head"), P("head", None), rows, P("seq"))
    return jax.shard_map(
        per_device, mesh=mesh, in_specs=in_specs, out_specs=(rows,) * 5, check_vma=False
    )
```

```python
import functools

import jax
import jax.numpy as jnp
from jax import lax
from jax.experimental import pallas as pl
from jax.experimental.pallas import tpu as pltpu
from jax.sharding import PartitionSpec as P

CG_STEPS = 4
EPSILON = 1e-06
LABEL_ROWS = 16
F32 = jnp.float32
BF16 = jnp.bfloat16
VMEM_LIMIT = 48 * 1024 * 1024
FLOPS_PER_US = 1e9
COT_US = 1.5
FINAL_US = 1.0
PAIR_JOIN_US = 5.0
MINE_US = 6.0
PAIR_US = 1.5
HALVE_US = 0.5


def mm(a, b):
    return lax.dot_general(a, b, (((1,), (0,)), ((), ())), preferred_element_type=F32)


def mm_nt(a, b):
    return lax.dot_general(a, b, (((1,), (1,)), ((), ())), preferred_element_type=F32)


def mm_tn(a, b):
    return lax.dot_general(a, b, (((0,), (0,)), ((), ())), preferred_element_type=F32)


def kernel_call(body, out_shape, operands, microseconds, name, smem=(), scratch=()):
    nbytes = sum(o.size * o.dtype.itemsize for o in operands)
    nbytes += sum(o.size * o.dtype.itemsize for o in out_shape)
    return pl.pallas_call(
        body,
        out_shape=out_shape,
        in_specs=[
            pl.BlockSpec(memory_space=pltpu.SMEM if i in smem else pltpu.VMEM)
            for i in range(len(operands))
        ],
        out_specs=[pl.BlockSpec(memory_space=pltpu.VMEM)] * len(out_shape),
        scratch_shapes=scratch,
        compiler_params=pltpu.CompilerParams(vmem_limit_bytes=VMEM_LIMIT),
        cost_estimate=pl.CostEstimate(
            flops=int(microseconds * FLOPS_PER_US), bytes_accessed=nbytes, transcendentals=0
        ),
        name=name,
    )(*operands)


def label_grids(rows_ref):
    piece = rows_ref.shape[0] - LABEL_ROWS
    labels = rows_ref[piece : piece + LABEL_ROWS, :piece].astype(F32)[0:1, :]
    across = jnp.broadcast_to(labels, (piece, piece))
    return piece, across, across.T


def document_mask(across, down):
    row = lax.broadcasted_iota(jnp.int32, across.shape, 0)
    col = lax.broadcasted_iota(jnp.int32, across.shape, 1)
    return (across == down) & (col <= row)


def triangle(width):
    row = lax.broadcasted_iota(jnp.int32, (width, width), 0)
    col = lax.broadcasted_iota(jnp.int32, (width, width), 1)
    return col < row, col == row


def unit_rows(width):
    return 3 * width + LABEL_ROWS


def pack_states(out_ref, label, full, symmetric):
    width = full[0].shape[0]
    below, diagonal = triangle(width)
    for unit in range(len(full) // 2):
        base = unit * unit_rows(width)
        for i in range(2):
            rows = slice(base + i * width, base + (i + 1) * width)
            out_ref[rows, :] = full[2 * unit + i].astype(BF16)
        one, two = symmetric[2 * unit], symmetric[2 * unit + 1]
        square = jnp.where(below | diagonal, one, two)
        out_ref[base + 2 * width : base + 3 * width, :] = square.astype(BF16)
        second = jnp.sum(jnp.where(diagonal, two, 0.0), axis=0, keepdims=True)
        rest = jnp.broadcast_to(label, (LABEL_ROWS - 1, width))
        out_ref[base + 3 * width : base + unit_rows(width), :] = jnp.concatenate(
            [second, rest], axis=0
        ).astype(BF16)


def join_units(near, far, width):
    near, far = near.astype(F32), far.astype(F32)
    size = unit_rows(width)
    joined = (near[size - 1 : size, :] == far[size - 1 : size, :]).astype(F32)
    number = lax.broadcasted_iota(jnp.int32, (LABEL_ROWS, width), 0) == 0
    parts = []
    for base in range(0, near.shape[0], size):
        body, rest = slice(base, base + 3 * width), slice(base + 3 * width, base + size)
        parts.append(near[body] + joined * far[body])
        parts.append(jnp.where(number, near[rest] + joined * far[rest], near[rest]))
    return jnp.concatenate(parts, axis=0)


def unpack_symmetric(square, row):
    below, diagonal = triangle(square.shape[0])
    flipped = square.T
    one = jnp.where(below | diagonal, square, flipped)
    two = jnp.where(diagonal, row, jnp.where(below, flipped, square))
    return one, two


def unpack_states(units, heads, width):
    size = unit_rows(width)
    label = units[size - 1 : size, :]
    full, symmetric = [], []
    for unit in range(heads // 2):
        part = units[unit * size : (unit + 1) * size, :]
        full += [part[:width].astype(BF16), part[width : 2 * width].astype(BF16)]
        square = part[2 * width : 3 * width]
        symmetric += [
            m.astype(BF16) for m in unpack_symmetric(square, part[3 * width : 3 * width + 1])
        ]
    return label, full, symmetric


def head_rows_of(rows_ref, heads, width, part, h):
    start = (part * heads + h) * width
    return rows_ref[: rows_ref.shape[0] - LABEL_ROWS, start : start + width]


def tail_body(heads, width, rows_ref, out_ref):
    piece, across, down = label_grids(rows_ref)
    last = jnp.max(across, axis=1, keepdims=True)
    tail = (down == last).astype(F32).astype(BF16)
    sums, grams = [], []
    for h in range(heads):
        key_h = head_rows_of(rows_ref, heads, width, 0, h)
        value_h = head_rows_of(rows_ref, heads, width, 1, h)
        masked = key_h * tail[:, :width]
        grams.append(mm_tn(key_h, masked))
        sums.append(mm_tn(value_h, masked))
    pack_states(out_ref, last[:1] + 1, sums, grams)


def cot_body(count, shard, place_ref, *refs):
    cots, weight_ref, cot_ref = refs[:count], refs[count], refs[count + 1]
    me = place_ref[1]
    total = None
    for b in range(count):
        owner = jnp.bitwise_xor(me, b)
        cols = pl.ds(pl.multiple_of(owner * shard, shard), shard)
        part = mm_nt(cots[b][...], weight_ref[:, cols])
        total = part if total is None else total + part
    cot_ref[...] = total.astype(BF16)


def project_body(count, shard, place_ref, mixed_ref, weight_ref, *refs):
    extras, keep_ref, send_ref = refs[:-2], refs[-2], refs[-1]
    piece = mixed_ref.shape[0]
    me = place_ref[1]
    mixed = mixed_ref[...]
    for c in range(count):
        owner = jnp.bitwise_xor(me, c)
        cols = pl.ds(pl.multiple_of(owner * shard, shard), shard)
        part = mm(mixed, weight_ref[:, cols])
        rows = slice(c // 2 * piece, (c // 2 + 1) * piece)
        if c % 2:
            send_ref[rows, :] = part.astype(BF16)
        else:
            keep_ref[rows, :] = part
    for i, extra in enumerate(extras):
        row = (count // 2 + i) * piece
        send_ref[row : row + piece, :] = extra[...]


def halve_body(blocks, piece, keep_ref, got_ref, rest_ref, send_ref):
    for c in range(blocks):
        rows = slice(c * piece, (c + 1) * piece)
        target = slice(c // 2 * piece, (c // 2 + 1) * piece)
        total = keep_ref[rows, :] + got_ref[rows, :].astype(F32)
        if c % 2:
            send_ref[target, :] = total.astype(BF16)
        else:
            rest_ref[target, :] = total


def join_body(width, near_ref, far_ref, *refs):
    out_ref = refs[-1]
    out_ref[...] = join_units(near_ref[...], far_ref[...], width).astype(BF16)


def pair_join_body(width, place_ref, here_ref, there_ref, out_ref):
    half = out_ref.shape[0]
    odd = lax.rem(place_ref[0], 2)
    mine = pl.ds(pl.multiple_of(odd * half, LABEL_ROWS), half)
    here, there = here_ref[mine, :].astype(F32), there_ref[mine, :].astype(F32)
    first, second = jnp.where(odd == 1, there, here), jnp.where(odd == 1, here, there)
    out_ref[...] = join_units(first, second, width).astype(BF16)


def pair_grad_body(piece, parts, arrays, by_place, place_ref, *refs):
    count = len(parts)
    cots, mixes = refs[:arrays], refs[arrays : arrays + count]
    kept_ref, given_ref, cot_ref, mix_ref, total_ref = refs[arrays + count :]
    for i, (array, row) in enumerate(parts):
        cot_at = jnp.bitwise_xor(place_ref[1], i) if by_place else i
        mix_at = jnp.bitwise_xor(lax.div(place_ref[0], 2), i) if by_place else i
        cot = cots[array][row : row + piece, :]
        cot_ref[pl.ds(pl.multiple_of(cot_at * piece, piece), piece), :] = cot
        mix_ref[pl.ds(pl.multiple_of(mix_at * piece, piece), piece), :] = mixes[i][...]
    total_ref[...] = mm_tn(cot_ref[...], mix_ref[...])
    half = kept_ref.shape[0]
    odd = lax.rem(place_ref[0], 2)
    kept_ref[...] = total_ref[pl.ds(pl.multiple_of(odd * half, half), half), :]
    given_ref[...] = total_ref[pl.ds(pl.multiple_of((1 - odd) * half, half), half), :].astype(BF16)


def solve_body(
    heads,
    width,
    ridge_ref,
    rows_ref,
    cot_ref,
    near_ref,
    far_ref,
    sol_ref,
    dual_ref,
    mixed_ref,
    out_ref,
):
    piece, across, down = label_grids(rows_ref)
    same = document_mask(across, down).astype(F32)
    same_two = jnp.concatenate([same, same], axis=0)
    first = jnp.min(across, axis=1, keepdims=True)
    head_rows = (down == first)[:, :width].astype(F32).astype(BF16)
    units = join_units(near_ref[...], far_ref[...], width)
    label, value_states, gram_states = unpack_states(units, heads, width)
    carried = ((down + 1)[:, :width] == label).astype(F32)
    carried_two = jnp.concatenate([carried, carried], axis=0)
    every = range(heads)
    keys = [head_rows_of(rows_ref, heads, width, 0, h) for h in every]
    values = [head_rows_of(rows_ref, heads, width, 1, h) for h in every]
    queries = [head_rows_of(rows_ref, heads, width, 2, h).astype(F32) for h in every]
    cots = [cot_ref[:, h * width : (h + 1) * width] for h in every]
    boths = [
        mm(cots[h], jnp.concatenate([values[h].T, value_states[h]], axis=1)) for h in every
    ]
    scores = [(both[:, :piece] * same).astype(BF16) for both in boths]
    targets = [carried * boths[h][:, piece:] + mm(scores[h], keys[h]) for h in every]
    rhs_keys = [jnp.concatenate([keys[h].T, gram_states[h]], axis=1) for h in every]
    directions = [jnp.concatenate([queries[h], targets[h]], axis=0) for h in every]
    residuals = directions
    solutions = [jnp.zeros_like(start) for start in directions]
    squares = [jnp.sum(start * start, axis=1, keepdims=True) for start in directions]
    for step in range(CG_STEPS):
        ps = directions
        boths = [mm(ps[h].astype(BF16), rhs_keys[h]) for h in range(heads)]
        scores = [(both[:, :piece] * same_two).astype(BF16) for both in boths]
        locals_ = [mm(scores[h], keys[h]) for h in range(heads)]
        applied = [
            carried_two * boths[h][:, piece:] + locals_[h] + ridge_ref[h] * ps[h]
            for h in range(heads)
        ]
        sizes = [squares[h] / (jnp.sum(ps[h] * applied[h], axis=1, keepdims=True) + EPSILON) for h in range(heads)]
        solutions = [solutions[h] + sizes[h] * ps[h] for h in range(heads)]
        if step + 1 < CG_STEPS:
            residuals = [residuals[h] - sizes[h] * applied[h] for h in range(heads)]
            news = [jnp.sum(residuals[h] * residuals[h], axis=1, keepdims=True) for h in range(heads)]
            directions = [
                residuals[h] + news[h] / (squares[h] + EPSILON) * ps[h] for h in range(heads)
            ]
            squares = news
    sols = [solutions[h][:piece].astype(BF16) for h in every]
    duals = [solutions[h][piece:].astype(BF16) for h in every]
    masked = [sol * head_rows for sol in sols]
    sums = [mm_tn(cots[h], masked[h]) for h in every]
    crosses = [mm_tn(duals[h], masked[h]) for h in every]
    boths = [
        mm(sols[h], jnp.concatenate([rhs_keys[h][:, :piece], value_states[h].T], axis=1))
        for h in every
    ]
    scores = [(both[:, :piece] * same).astype(BF16) for both in boths]
    outputs = [carried * boths[h][:, piece:] + mm(scores[h], values[h]) for h in every]
    for h in every:
        cols = slice(h * width, (h + 1) * width)
        mixed_ref[:, cols] = outputs[h].astype(BF16)
        sol_ref[:, cols] = sols[h]
        dual_ref[:, cols] = duals[h]
    pack_states(out_ref, first[:1] + 1, sums, [cross + cross.T for cross in crosses])


def local_grads_body(
    heads, width, rows_ref, cot_ref, sol_ref, dual_ref, grad_k_ref, grad_v_ref
):
    piece, across, down = label_grids(rows_ref)
    same = document_mask(across, down).astype(F32)
    same_two = jnp.concatenate([same, same], axis=0)
    for h in range(heads):
        cols = slice(h * width, (h + 1) * width)
        key_h = head_rows_of(rows_ref, heads, width, 0, h)
        value_h = head_rows_of(rows_ref, heads, width, 1, h)
        cot_h = cot_ref[:, cols]
        sol, dual = sol_ref[:, cols], dual_ref[:, cols]
        score_two = (mm_nt(cot_h, value_h) * same).astype(BF16)
        pair = (mm_nt(jnp.concatenate([sol, dual], axis=0), key_h) * same_two).astype(BF16)
        score_one, score_three = pair[:piece], pair[piece:]
        grad_v_ref[:, cols] = mm_tn(score_one, cot_h)
        grad_k_ref[:, cols] = mm_tn(
            jnp.concatenate([score_two, -score_three, -score_one], axis=0),
            jnp.concatenate([sol, sol, dual], axis=0),
        )


def final_grads_body(
    heads,
    width,
    place_ref,
    rows_ref,
    there_ref,
    mine_ref,
    theirs_ref,
    local_k_ref,
    local_v_ref,
    grad_k_ref,
    grad_v_ref,
    later_ref,
):
    piece, _, down = label_grids(rows_ref)
    half = mine_ref.shape[0]
    odd = lax.rem(place_ref[0], 2)
    later_ref[pl.ds(pl.multiple_of(odd * half, LABEL_ROWS), half), :] = mine_ref[...]
    later_ref[pl.ds(pl.multiple_of((1 - odd) * half, LABEL_ROWS), half), :] = theirs_ref[...]
    units = jnp.where(
        odd == 1,
        later_ref[...].astype(F32),
        join_units(there_ref[...], later_ref[...], width),
    )
    label, grad_states, gram_grads = unpack_states(units, heads, width)
    later = ((down + 1)[:, :width] == label).astype(F32)
    every = range(heads)
    keys = [head_rows_of(rows_ref, heads, width, 0, h) for h in every]
    values = [head_rows_of(rows_ref, heads, width, 1, h) for h in every]
    from_values = [mm_nt(keys[h], grad_states[h]) for h in every]
    from_keys = [mm(values[h], grad_states[h]) - mm(keys[h], gram_grads[h]) for h in every]
    for h in every:
        cols = slice(h * width, (h + 1) * width)
        grad_v_ref[:, cols] = (local_v_ref[:, cols] + later * from_values[h]).astype(BF16)
        grad_k_ref[:, cols] = (local_k_ref[:, cols] + later * from_keys[h]).astype(BF16)


def rotated(value, by):
    devices = lax.axis_size("seq")
    return lax.ppermute(value, "seq", [(i, (i + by) % devices) for i in range(devices)])


def swapped(value, axis, mask):
    devices = lax.axis_size(axis)
    return lax.ppermute(value, axis, [(i, i ^ mask) for i in range(devices)])


def joined_inputs(key_rows, value_rows, query_rows, doc_row):
    piece, features = key_rows.shape
    parts = (key_rows, value_rows, query_rows)
    width = len(parts) * features
    total = jnp.pad(
        doc_row.astype(BF16), ((piece, LABEL_ROWS - 1), (0, width - doc_row.shape[1]))
    )
    for i, part in enumerate(parts):
        total += jnp.pad(part, ((0, LABEL_ROWS), (i * features, width - (i + 1) * features)))
    return total


def join_states(near, far, width, *after):
    (joined,) = kernel_call(
        functools.partial(join_body, width),
        [jax.ShapeDtypeStruct(far.shape, BF16)],
        (near, far, *after),
        MINE_US if after else 0.5,
        "join_states",
    )
    return joined


def per_device(query_rows, key_rows, value_rows, ridge_reg, out_weight, out_grad, doc_ids):
    heads = ridge_reg.shape[0]
    piece, features = key_rows.shape
    width = features // heads
    seq_size, head_size = lax.axis_size("seq"), lax.axis_size("head")
    seq_at, head_at = lax.axis_index("seq"), lax.axis_index("head")
    place = jnp.stack([seq_at, head_at]).astype(jnp.int32)
    model = out_weight.shape[1]
    shard = model // head_size
    doc_row = doc_ids.reshape(1, piece)
    payload = jax.ShapeDtypeStruct((heads // 2 * unit_rows(width), width), BF16)
    half_payload = jax.ShapeDtypeStruct((payload.shape[0] // 2, width), BF16)
    rows_bf16 = jax.ShapeDtypeStruct((piece, features), BF16)
    rows_f32 = jax.ShapeDtypeStruct((piece, features), F32)
    window = seq_size // 2
    pairs = seq_size // 2
    pair_rows = model // pairs
    pair_at = seq_at // 2
    square = pairs == head_size

    rows_in = joined_inputs(key_rows, value_rows, query_rows, doc_row)
    (element,) = kernel_call(
        functools.partial(tail_body, heads, width),
        [payload],
        (rows_in,),
        0.5,
        "tail_states",
    )
    near, far, reach = rotated(element, 1), rotated(element, 2), 2
    cots = [out_grad] + [swapped(out_grad, "head", b) for b in range(1, head_size)]
    near, far, cots = lax.optimization_barrier((near, far, cots))
    while reach < window:
        near = join_states(near, far, width)
        far = rotated(near, reach)
        reach *= 2
    near, cot_here = lax.optimization_barrier((near, out_grad))
    if square:
        turned = lax.ppermute(
            cot_here,
            ("seq", "head"),
            [
                ((2 * z + y) * head_size + h, (2 * h + y) * head_size + z)
                for z in range(pairs)
                for y in range(2)
                for h in range(head_size)
            ],
        )
    else:
        turned = cot_here

    (out_cot,) = kernel_call(
        functools.partial(cot_body, head_size, shard),
        [rows_bf16],
        (place, *cots, out_weight),
        1.5,
        "cotangent",
        smem=(0,),
    )
    sol, dual, mixed, back = kernel_call(
        functools.partial(solve_body, heads, width),
        [rows_bf16, rows_bf16, rows_bf16, payload],
        (ridge_reg, rows_in, out_cot, near, far),
        5.0,
        "solve",
        smem=(0,),
    )
    mixes = [mixed] + [None] * (pairs - 1)
    for step in range(1, pairs):
        if not square:
            mixes[step] = rotated(mixed, -2 * step)
        elif step & (step - 1) == 0:
            mixes[step] = swapped(mixed, "seq", 2 * step)
    there = swapped(back, "seq", 1)
    (pair_half,) = kernel_call(
        functools.partial(pair_join_body, width),
        [half_payload],
        (place, back, there),
        PAIR_JOIN_US,
        "pair_join",
        smem=(0,),
    )
    ready, turned = lax.optimization_barrier((mixed, turned))
    even_blocks, mask = {0: turned}, 2
    while square and mask < head_size:
        for i in list(even_blocks):
            even_blocks[i | mask] = swapped(even_blocks[i], "head", mask)
        mask *= 2
    even_blocks = [even_blocks[i] for i in sorted(even_blocks)]
    blocks = head_size // 2
    keep, send = kernel_call(
        functools.partial(project_body, head_size, shard),
        [
            jax.ShapeDtypeStruct((blocks * piece, shard), F32),
            jax.ShapeDtypeStruct(((blocks + len(even_blocks)) * piece, shard), BF16),
        ],
        (place, ready, out_weight, *even_blocks),
        1.0,
        "project",
        smem=(0,),
    )
    got, mask = swapped(send, "head", 1), 2
    held = {i: mixes[i] for i in range(1, pairs) if mixes[i] is not None and i % 2 == 0}
    held, got, after = lax.optimization_barrier((held, got, pair_half))
    near, far, reach = rotated(pair_half, -2), rotated(pair_half, -4), 4
    while reach < window:
        near = join_states(near, far, width)
        far = rotated(near, -reach)
        reach *= 2
    mine = join_states(near, far, width, after)
    theirs = swapped(mine, "seq", 1)
    for step in range(1, pairs):
        low = step & -step
        if mixes[step] is None:
            held[step] = mixes[step] = swapped(held[step ^ low], "seq", 2 * low)

    gathered = [*even_blocks, got]
    parts = []
    for i in range(len(even_blocks)):
        parts += [(i, 0), (len(even_blocks), (blocks + i) * piece)]
    while blocks > 1:
        blocks //= 2
        keep, send = kernel_call(
            functools.partial(halve_body, 2 * blocks, piece),
            [
                jax.ShapeDtypeStruct((blocks * piece, shard), F32),
                jax.ShapeDtypeStruct((blocks * piece, shard), BF16),
            ],
            (keep, got),
            0.5,
            "halve",
        )
        got = swapped(send, "head", mask)
        mask *= 2
    layer_out = (keep + got[:piece].astype(F32)).astype(BF16)
    if not square:
        cot_full = lax.all_gather(out_grad, "head", axis=1, tiled=True)
        gathered = []
        for step in range(pairs):
            start = lax.rem(pair_at + pairs - step, pairs) * pair_rows
            block = lax.dynamic_slice_in_dim(cot_full, start, pair_rows, 1)
            gathered.append(rotated(block, -2 * step) if step else block)
        parts = [(step, 0) for step in range(pairs)]

    kept, given = kernel_call(
        functools.partial(pair_grad_body, piece, tuple(parts), len(gathered), square),
        [
            jax.ShapeDtypeStruct((pair_rows // 2, features), F32),
            jax.ShapeDtypeStruct((pair_rows // 2, features), BF16),
        ],
        (place, *gathered, *mixes),
        PAIR_US,
        "pair_grad",
        smem=(0,),
        scratch=[
            pltpu.VMEM((pairs * piece, pair_rows), BF16),
            pltpu.VMEM((pairs * piece, features), BF16),
            pltpu.VMEM((pair_rows, features), F32),
        ],
    )
    grad_weight = kept + swapped(given, "seq", 1).astype(F32)

    local_k, local_v = kernel_call(
        functools.partial(local_grads_body, heads, width),
        [rows_f32, rows_f32],
        (rows_in, out_cot, sol, dual),
        1.1,
        "local_grads",
    )
    grad_keys, grad_values = kernel_call(
        functools.partial(final_grads_body, heads, width),
        [rows_bf16, rows_bf16],
        (place, rows_in, there, mine, theirs, local_k, local_v),
        FINAL_US,
        "final_grads",
        smem=(0,),
        scratch=[pltpu.VMEM(payload.shape, BF16)],
    )
    return (layer_out, dual, grad_keys, grad_values, grad_weight)


def solution(mesh):
    rows = P("seq", "head")
    in_specs = (rows, rows, rows, P("head"), P("head", None), rows, P("seq"))
    return jax.shard_map(
        per_device, mesh=mesh, in_specs=in_specs, out_specs=(rows,) * 5, check_vma=False
    )
```

```python
import functools

import jax
import jax.numpy as jnp
from jax import lax
from jax.experimental import pallas as pl
from jax.experimental.pallas import tpu as pltpu
from jax.sharding import PartitionSpec as P

CG_STEPS = 4
EPSILON = 1e-06
LABEL_ROWS = 16
F32 = jnp.float32
BF16 = jnp.bfloat16
VMEM_LIMIT = 48 * 1024 * 1024
FLOPS_PER_US = 1e9
COT_US = 1.5
FINAL_US = 1.0
PAIR_JOIN_US = 5.0
MINE_US = 12.0
PAIR_US = 1.5
HALVE_US = 0.5


def mm(a, b):
    return lax.dot_general(a, b, (((1,), (0,)), ((), ())), preferred_element_type=F32)


def mm_nt(a, b):
    return lax.dot_general(a, b, (((1,), (1,)), ((), ())), preferred_element_type=F32)


def mm_tn(a, b):
    return lax.dot_general(a, b, (((0,), (0,)), ((), ())), preferred_element_type=F32)


def kernel_call(body, out_shape, operands, microseconds, name, smem=(), scratch=()):
    nbytes = sum(o.size * o.dtype.itemsize for o in operands)
    nbytes += sum(o.size * o.dtype.itemsize for o in out_shape)
    return pl.pallas_call(
        body,
        out_shape=out_shape,
        in_specs=[
            pl.BlockSpec(memory_space=pltpu.SMEM if i in smem else pltpu.VMEM)
            for i in range(len(operands))
        ],
        out_specs=[pl.BlockSpec(memory_space=pltpu.VMEM)] * len(out_shape),
        scratch_shapes=scratch,
        compiler_params=pltpu.CompilerParams(vmem_limit_bytes=VMEM_LIMIT),
        cost_estimate=pl.CostEstimate(
            flops=int(microseconds * FLOPS_PER_US), bytes_accessed=nbytes, transcendentals=0
        ),
        name=name,
    )(*operands)


def label_grids(rows_ref):
    piece = rows_ref.shape[0] - LABEL_ROWS
    labels = rows_ref[piece : piece + LABEL_ROWS, :piece].astype(F32)[0:1, :]
    across = jnp.broadcast_to(labels, (piece, piece))
    return piece, across, across.T


def document_mask(across, down):
    row = lax.broadcasted_iota(jnp.int32, across.shape, 0)
    col = lax.broadcasted_iota(jnp.int32, across.shape, 1)
    return (across == down) & (col <= row)


def triangle(width):
    row = lax.broadcasted_iota(jnp.int32, (width, width), 0)
    col = lax.broadcasted_iota(jnp.int32, (width, width), 1)
    return col < row, col == row


def unit_rows(width):
    return 3 * width + LABEL_ROWS


def pack_states(out_ref, label, full, symmetric):
    width = full[0].shape[0]
    below, diagonal = triangle(width)
    for unit in range(len(full) // 2):
        base = unit * unit_rows(width)
        for i in range(2):
            rows = slice(base + i * width, base + (i + 1) * width)
            out_ref[rows, :] = full[2 * unit + i].astype(BF16)
        one, two = symmetric[2 * unit], symmetric[2 * unit + 1]
        square = jnp.where(below | diagonal, one, two)
        out_ref[base + 2 * width : base + 3 * width, :] = square.astype(BF16)
        second = jnp.sum(jnp.where(diagonal, two, 0.0), axis=0, keepdims=True)
        rest = jnp.broadcast_to(label, (LABEL_ROWS - 1, width))
        out_ref[base + 3 * width : base + unit_rows(width), :] = jnp.concatenate(
            [second, rest], axis=0
        ).astype(BF16)


def join_units(near, far, width):
    near, far = near.astype(F32), far.astype(F32)
    size = unit_rows(width)
    joined = (near[size - 1 : size, :] == far[size - 1 : size, :]).astype(F32)
    number = lax.broadcasted_iota(jnp.int32, (LABEL_ROWS, width), 0) == 0
    parts = []
    for base in range(0, near.shape[0], size):
        body, rest = slice(base, base + 3 * width), slice(base + 3 * width, base + size)
        parts.append(near[body] + joined * far[body])
        parts.append(jnp.where(number, near[rest] + joined * far[rest], near[rest]))
    return jnp.concatenate(parts, axis=0)


def unpack_symmetric(square, row):
    below, diagonal = triangle(square.shape[0])
    flipped = square.T
    one = jnp.where(below | diagonal, square, flipped)
    two = jnp.where(diagonal, row, jnp.where(below, flipped, square))
    return one, two


def unpack_states(units, heads, width):
    size = unit_rows(width)
    label = units[size - 1 : size, :]
    full, symmetric = [], []
    for unit in range(heads // 2):
        part = units[unit * size : (unit + 1) * size, :]
        full += [part[:width].astype(BF16), part[width : 2 * width].astype(BF16)]
        square = part[2 * width : 3 * width]
        symmetric += [
            m.astype(BF16) for m in unpack_symmetric(square, part[3 * width : 3 * width + 1])
        ]
    return label, full, symmetric


def head_rows_of(rows_ref, heads, width, part, h):
    start = (part * heads + h) * width
    return rows_ref[: rows_ref.shape[0] - LABEL_ROWS, start : start + width]


def tail_body(heads, width, rows_ref, out_ref):
    piece, across, down = label_grids(rows_ref)
    last = jnp.max(across, axis=1, keepdims=True)
    tail = (down == last).astype(F32).astype(BF16)
    sums, grams = [], []
    for h in range(heads):
        key_h = head_rows_of(rows_ref, heads, width, 0, h)
        value_h = head_rows_of(rows_ref, heads, width, 1, h)
        masked = key_h * tail[:, :width]
        grams.append(mm_tn(key_h, masked))
        sums.append(mm_tn(value_h, masked))
    pack_states(out_ref, last[:1] + 1, sums, grams)


def cot_body(count, shard, place_ref, *refs):
    cots, weight_ref, cot_ref = refs[:count], refs[count], refs[count + 1]
    me = place_ref[1]
    total = None
    for b in range(count):
        owner = jnp.bitwise_xor(me, b)
        cols = pl.ds(pl.multiple_of(owner * shard, shard), shard)
        part = mm_nt(cots[b][...], weight_ref[:, cols])
        total = part if total is None else total + part
    cot_ref[...] = total.astype(BF16)


def project_body(count, shard, place_ref, mixed_ref, weight_ref, *refs):
    extras, keep_ref, send_ref = refs[:-2], refs[-2], refs[-1]
    piece = mixed_ref.shape[0]
    me = place_ref[1]
    mixed = mixed_ref[...]
    for c in range(count):
        owner = jnp.bitwise_xor(me, c)
        cols = pl.ds(pl.multiple_of(owner * shard, shard), shard)
        part = mm(mixed, weight_ref[:, cols])
        rows = slice(c // 2 * piece, (c // 2 + 1) * piece)
        if c % 2:
            send_ref[rows, :] = part.astype(BF16)
        else:
            keep_ref[rows, :] = part
    for i, extra in enumerate(extras):
        row = (count // 2 + i) * piece
        send_ref[row : row + piece, :] = extra[...]


def halve_body(blocks, piece, keep_ref, got_ref, rest_ref, send_ref):
    for c in range(blocks):
        rows = slice(c * piece, (c + 1) * piece)
        target = slice(c // 2 * piece, (c // 2 + 1) * piece)
        total = keep_ref[rows, :] + got_ref[rows, :].astype(F32)
        if c % 2:
            send_ref[target, :] = total.astype(BF16)
        else:
            rest_ref[target, :] = total


def join_body(width, near_ref, far_ref, *refs):
    out_ref = refs[-1]
    out_ref[...] = join_units(near_ref[...], far_ref[...], width).astype(BF16)


def pair_join_body(width, place_ref, here_ref, there_ref, out_ref):
    half = out_ref.shape[0]
    odd = lax.rem(place_ref[0], 2)
    mine = pl.ds(pl.multiple_of(odd * half, LABEL_ROWS), half)
    here, there = here_ref[mine, :].astype(F32), there_ref[mine, :].astype(F32)
    first, second = jnp.where(odd == 1, there, here), jnp.where(odd == 1, here, there)
    out_ref[...] = join_units(first, second, width).astype(BF16)


def pair_grad_body(piece, parts, arrays, by_place, place_ref, *refs):
    count = len(parts)
    cots, mixes = refs[:arrays], refs[arrays : arrays + count]
    kept_ref, given_ref, cot_ref, mix_ref, total_ref = refs[arrays + count :]
    for i, (array, row) in enumerate(parts):
        cot_at = jnp.bitwise_xor(place_ref[1], i) if by_place else i
        mix_at = jnp.bitwise_xor(lax.div(place_ref[0], 2), i) if by_place else i
        cot = cots[array][row : row + piece, :]
        cot_ref[pl.ds(pl.multiple_of(cot_at * piece, piece), piece), :] = cot
        mix_ref[pl.ds(pl.multiple_of(mix_at * piece, piece), piece), :] = mixes[i][...]
    total_ref[...] = mm_tn(cot_ref[...], mix_ref[...])
    half = kept_ref.shape[0]
    odd = lax.rem(place_ref[0], 2)
    kept_ref[...] = total_ref[pl.ds(pl.multiple_of(odd * half, half), half), :]
    given_ref[...] = total_ref[pl.ds(pl.multiple_of((1 - odd) * half, half), half), :].astype(BF16)


def solve_body(
    heads,
    width,
    ridge_ref,
    rows_ref,
    cot_ref,
    near_ref,
    far_ref,
    sol_ref,
    dual_ref,
    mixed_ref,
    out_ref,
):
    piece, across, down = label_grids(rows_ref)
    same = document_mask(across, down).astype(F32).astype(BF16)
    same_two = jnp.concatenate([same, same], axis=0)
    first = jnp.min(across, axis=1, keepdims=True)
    head_rows = (down == first)[:, :width].astype(F32).astype(BF16)
    units = join_units(near_ref[...], far_ref[...], width)
    label, value_states, gram_states = unpack_states(units, heads, width)
    carried = ((down + 1)[:, :width] == label).astype(F32).astype(BF16)
    carried_two = jnp.concatenate([carried, carried], axis=0)
    every = range(heads)
    keys = [head_rows_of(rows_ref, heads, width, 0, h) for h in every]
    values = [head_rows_of(rows_ref, heads, width, 1, h) for h in every]
    queries = [head_rows_of(rows_ref, heads, width, 2, h).astype(F32) for h in every]
    cots = [cot_ref[:, h * width : (h + 1) * width] for h in every]
    keys_across = [key.T for key in keys]
    scores = [mm(cots[h], values[h].T).astype(BF16) * same for h in every]
    targets = [
        mm(
            jnp.concatenate([scores[h], cots[h] * carried], axis=1),
            jnp.concatenate([keys[h], value_states[h]], axis=0),
        )
        for h in every
    ]
    systems = [jnp.concatenate([keys[h], gram_states[h]], axis=0) for h in every]
    directions = [jnp.concatenate([queries[h], targets[h]], axis=0) for h in every]
    residuals = directions
    solutions = [jnp.zeros_like(start) for start in directions]
    squares = [jnp.sum(start * start, axis=1, keepdims=True) for start in directions]
    for step in range(CG_STEPS):
        ps = directions
        rounded = [p.astype(BF16) for p in ps]
        scores = [mm(rounded[h], keys_across[h]).astype(BF16) * same_two for h in every]
        lefts = [
            jnp.concatenate([scores[h], rounded[h] * carried_two], axis=1) for h in every
        ]
        applied = [mm(lefts[h], systems[h]) + ridge_ref[h] * ps[h] for h in every]
        sizes = [squares[h] / (jnp.sum(ps[h] * applied[h], axis=1, keepdims=True) + EPSILON) for h in range(heads)]
        solutions = [solutions[h] + sizes[h] * ps[h] for h in range(heads)]
        if step + 1 < CG_STEPS:
            residuals = [residuals[h] - sizes[h] * applied[h] for h in range(heads)]
            news = [jnp.sum(residuals[h] * residuals[h], axis=1, keepdims=True) for h in range(heads)]
            directions = [
                residuals[h] + news[h] / (squares[h] + EPSILON) * ps[h] for h in range(heads)
            ]
            squares = news
    sols = [solutions[h][:piece].astype(BF16) for h in every]
    duals = [solutions[h][piece:].astype(BF16) for h in every]
    masked = [sol * head_rows for sol in sols]
    sums = [mm_tn(cots[h], masked[h]) for h in every]
    crosses = [mm_tn(duals[h], masked[h]) for h in every]
    scores = [mm(sols[h], keys_across[h]).astype(BF16) * same for h in every]
    outputs = [
        mm(
            jnp.concatenate([scores[h], sols[h] * carried], axis=1),
            jnp.concatenate([values[h], value_states[h].T], axis=0),
        )
        for h in every
    ]
    for h in every:
        cols = slice(h * width, (h + 1) * width)
        mixed_ref[:, cols] = outputs[h].astype(BF16)
        sol_ref[:, cols] = sols[h]
        dual_ref[:, cols] = duals[h]
    pack_states(out_ref, first[:1] + 1, sums, [cross + cross.T for cross in crosses])


def local_grads_body(
    heads, width, rows_ref, cot_ref, sol_ref, dual_ref, grad_k_ref, grad_v_ref
):
    piece, across, down = label_grids(rows_ref)
    same = document_mask(across, down).astype(F32)
    same_two = jnp.concatenate([same, same], axis=0)
    for h in range(heads):
        cols = slice(h * width, (h + 1) * width)
        key_h = head_rows_of(rows_ref, heads, width, 0, h)
        value_h = head_rows_of(rows_ref, heads, width, 1, h)
        cot_h = cot_ref[:, cols]
        sol, dual = sol_ref[:, cols], dual_ref[:, cols]
        score_two = (mm_nt(cot_h, value_h) * same).astype(BF16)
        pair = (mm_nt(jnp.concatenate([sol, dual], axis=0), key_h) * same_two).astype(BF16)
        score_one, score_three = pair[:piece], pair[piece:]
        grad_v_ref[:, cols] = mm_tn(score_one, cot_h)
        grad_k_ref[:, cols] = mm_tn(
            jnp.concatenate([score_two, -score_three, -score_one], axis=0),
            jnp.concatenate([sol, sol, dual], axis=0),
        )


def final_grads_body(
    heads,
    width,
    place_ref,
    rows_ref,
    there_ref,
    mine_ref,
    theirs_ref,
    local_k_ref,
    local_v_ref,
    grad_k_ref,
    grad_v_ref,
    later_ref,
):
    piece, _, down = label_grids(rows_ref)
    half = mine_ref.shape[0]
    odd = lax.rem(place_ref[0], 2)
    later_ref[pl.ds(pl.multiple_of(odd * half, LABEL_ROWS), half), :] = mine_ref[...]
    later_ref[pl.ds(pl.multiple_of((1 - odd) * half, LABEL_ROWS), half), :] = theirs_ref[...]
    units = jnp.where(
        odd == 1,
        later_ref[...].astype(F32),
        join_units(there_ref[...], later_ref[...], width),
    )
    label, grad_states, gram_grads = unpack_states(units, heads, width)
    later = ((down + 1)[:, :width] == label).astype(F32)
    every = range(heads)
    keys = [head_rows_of(rows_ref, heads, width, 0, h) for h in every]
    values = [head_rows_of(rows_ref, heads, width, 1, h) for h in every]
    from_values = [mm_nt(keys[h], grad_states[h]) for h in every]
    from_keys = [mm(values[h], grad_states[h]) - mm(keys[h], gram_grads[h]) for h in every]
    for h in every:
        cols = slice(h * width, (h + 1) * width)
        grad_v_ref[:, cols] = (local_v_ref[:, cols] + later * from_values[h]).astype(BF16)
        grad_k_ref[:, cols] = (local_k_ref[:, cols] + later * from_keys[h]).astype(BF16)


def rotated(value, by):
    devices = lax.axis_size("seq")
    return lax.ppermute(value, "seq", [(i, (i + by) % devices) for i in range(devices)])


def swapped(value, axis, mask):
    devices = lax.axis_size(axis)
    return lax.ppermute(value, axis, [(i, i ^ mask) for i in range(devices)])


def joined_inputs(key_rows, value_rows, query_rows, doc_row):
    piece, features = key_rows.shape
    parts = (key_rows, value_rows, query_rows)
    width = len(parts) * features
    total = jnp.pad(
        doc_row.astype(BF16), ((piece, LABEL_ROWS - 1), (0, width - doc_row.shape[1]))
    )
    for i, part in enumerate(parts):
        total += jnp.pad(part, ((0, LABEL_ROWS), (i * features, width - (i + 1) * features)))
    return total


def join_states(near, far, width, *after):
    (joined,) = kernel_call(
        functools.partial(join_body, width),
        [jax.ShapeDtypeStruct(far.shape, BF16)],
        (near, far, *after),
        MINE_US if after else 0.5,
        "join_states",
    )
    return joined


def per_device(query_rows, key_rows, value_rows, ridge_reg, out_weight, out_grad, doc_ids):
    heads = ridge_reg.shape[0]
    piece, features = key_rows.shape
    width = features // heads
    seq_size, head_size = lax.axis_size("seq"), lax.axis_size("head")
    seq_at, head_at = lax.axis_index("seq"), lax.axis_index("head")
    place = jnp.stack([seq_at, head_at]).astype(jnp.int32)
    model = out_weight.shape[1]
    shard = model // head_size
    doc_row = doc_ids.reshape(1, piece)
    payload = jax.ShapeDtypeStruct((heads // 2 * unit_rows(width), width), BF16)
    half_payload = jax.ShapeDtypeStruct((payload.shape[0] // 2, width), BF16)
    rows_bf16 = jax.ShapeDtypeStruct((piece, features), BF16)
    rows_f32 = jax.ShapeDtypeStruct((piece, features), F32)
    window = seq_size // 2
    pairs = seq_size // 2
    pair_rows = model // pairs
    pair_at = seq_at // 2
    square = pairs == head_size

    rows_in = joined_inputs(key_rows, value_rows, query_rows, doc_row)
    (element,) = kernel_call(
        functools.partial(tail_body, heads, width),
        [payload],
        (rows_in,),
        0.5,
        "tail_states",
    )
    near, far, reach = rotated(element, 1), rotated(element, 2), 2
    cots = [out_grad] + [swapped(out_grad, "head", b) for b in range(1, head_size)]
    near, far, cots = lax.optimization_barrier((near, far, cots))
    while reach < window:
        near = join_states(near, far, width)
        far = rotated(near, reach)
        reach *= 2
    near, cot_here = lax.optimization_barrier((near, out_grad))
    if square:
        turned = lax.ppermute(
            cot_here,
            ("seq", "head"),
            [
                ((2 * z + y) * head_size + h, (2 * h + y) * head_size + z)
                for z in range(pairs)
                for y in range(2)
                for h in range(head_size)
            ],
        )
    else:
        turned = cot_here

    (out_cot,) = kernel_call(
        functools.partial(cot_body, head_size, shard),
        [rows_bf16],
        (place, *cots, out_weight),
        1.5,
        "cotangent",
        smem=(0,),
    )
    sol, dual, mixed, back = kernel_call(
        functools.partial(solve_body, heads, width),
        [rows_bf16, rows_bf16, rows_bf16, payload],
        (ridge_reg, rows_in, out_cot, near, far),
        5.0,
        "solve",
        smem=(0,),
    )
    mixes = [mixed] + [None] * (pairs - 1)
    for step in range(1, pairs):
        if not square:
            mixes[step] = rotated(mixed, -2 * step)
        elif step & (step - 1) == 0:
            mixes[step] = swapped(mixed, "seq", 2 * step)
    there = swapped(back, "seq", 1)
    (pair_half,) = kernel_call(
        functools.partial(pair_join_body, width),
        [half_payload],
        (place, back, there),
        PAIR_JOIN_US,
        "pair_join",
        smem=(0,),
    )
    ready, turned = lax.optimization_barrier((mixed, turned))
    even_blocks, mask = {0: turned}, 2
    while square and mask < head_size:
        for i in list(even_blocks):
            even_blocks[i | mask] = swapped(even_blocks[i], "head", mask)
        mask *= 2
    even_blocks = [even_blocks[i] for i in sorted(even_blocks)]
    blocks = head_size // 2
    keep, send = kernel_call(
        functools.partial(project_body, head_size, shard),
        [
            jax.ShapeDtypeStruct((blocks * piece, shard), F32),
            jax.ShapeDtypeStruct(((blocks + len(even_blocks)) * piece, shard), BF16),
        ],
        (place, ready, out_weight, *even_blocks),
        0.05,
        "project",
        smem=(0,),
    )
    got, mask = swapped(send, "head", 1), 2
    held = {i: mixes[i] for i in range(1, pairs) if mixes[i] is not None and i % 2 == 0}
    held, got, after = lax.optimization_barrier((held, got, pair_half))
    near, far, reach = rotated(pair_half, -2), rotated(pair_half, -4), 4
    while reach < window:
        near = join_states(near, far, width)
        far = rotated(near, -reach)
        reach *= 2
    mine = join_states(near, far, width, after)
    theirs = swapped(mine, "seq", 1)
    for step in range(1, pairs):
        low = step & -step
        if mixes[step] is None:
            held[step] = mixes[step] = swapped(held[step ^ low], "seq", 2 * low)

    gathered = [*even_blocks, got]
    parts = []
    for i in range(len(even_blocks)):
        parts += [(i, 0), (len(even_blocks), (blocks + i) * piece)]
    while blocks > 1:
        blocks //= 2
        keep, send = kernel_call(
            functools.partial(halve_body, 2 * blocks, piece),
            [
                jax.ShapeDtypeStruct((blocks * piece, shard), F32),
                jax.ShapeDtypeStruct((blocks * piece, shard), BF16),
            ],
            (keep, got),
            0.5,
            "halve",
        )
        got = swapped(send, "head", mask)
        mask *= 2
    layer_out = (keep + got[:piece].astype(F32)).astype(BF16)
    if not square:
        cot_full = lax.all_gather(out_grad, "head", axis=1, tiled=True)
        gathered = []
        for step in range(pairs):
            start = lax.rem(pair_at + pairs - step, pairs) * pair_rows
            block = lax.dynamic_slice_in_dim(cot_full, start, pair_rows, 1)
            gathered.append(rotated(block, -2 * step) if step else block)
        parts = [(step, 0) for step in range(pairs)]

    kept, given = kernel_call(
        functools.partial(pair_grad_body, piece, tuple(parts), len(gathered), square),
        [
            jax.ShapeDtypeStruct((pair_rows // 2, features), F32),
            jax.ShapeDtypeStruct((pair_rows // 2, features), BF16),
        ],
        (place, *gathered, *mixes),
        PAIR_US,
        "pair_grad",
        smem=(0,),
        scratch=[
            pltpu.VMEM((pairs * piece, pair_rows), BF16),
            pltpu.VMEM((pairs * piece, features), BF16),
            pltpu.VMEM((pair_rows, features), F32),
        ],
    )
    grad_weight = kept + swapped(given, "seq", 1).astype(F32)

    local_k, local_v = kernel_call(
        functools.partial(local_grads_body, heads, width),
        [rows_f32, rows_f32],
        (rows_in, out_cot, sol, dual),
        1.1,
        "local_grads",
    )
    grad_keys, grad_values = kernel_call(
        functools.partial(final_grads_body, heads, width),
        [rows_bf16, rows_bf16],
        (place, rows_in, there, mine, theirs, local_k, local_v),
        FINAL_US,
        "final_grads",
        smem=(0,),
        scratch=[pltpu.VMEM(payload.shape, BF16)],
    )
    return (layer_out, dual, grad_keys, grad_values, grad_weight)


def solution(mesh):
    rows = P("seq", "head")
    in_specs = (rows, rows, rows, P("head"), P("head", None), rows, P("seq"))
    return jax.shard_map(
        per_device, mesh=mesh, in_specs=in_specs, out_specs=(rows,) * 5, check_vma=False
    )
```
